32 devices in a mesh: prow: 4 (over y, x), pcol: 8 (over z, core).
Axes of the slice: x: 2, y: 2, z: 4, core: 2. Of those that a mesh axis runs over, the one named last changes fastest.
Arguments:
- coupling: float32 [16, 512, 8, 1024], P(None, 'prow', None, 'pcol'), as said below
- diagonal: float32 [16, 512], P(None, 'prow'), as said below
Outputs:
- trailing: float32 [16, 512, 8, 1024], P(None, 'prow', None, 'pcol')
Inputs may be any that keep to these rules, and one draw needn't show every extreme that they name: coupling read as in the reference program is symmetric, and coupling plus diag(diagonal) is symmetric positive definite. `diagonal`: every entry is positive.
All inputs are finite; a program needn't handle non-finite values.
Results may differ from the reference program's by a relative error of at most 0.00005.
Values sent between devices are 32-bit elements; how exact they have to be, the bound alone decides.
A program may use at most 128 MiB of HBM per device.

```python
import jax
import jax.numpy as jnp
from jax import lax

NB = 128
MB = 64
N_PROW = 4
N_PCOL = 8


def row_scales(key, top):
    order = MB * NB
    base = jax.random.uniform(jax.random.fold_in(key, 11), (order,), jnp.float32)
    return jnp.exp(base * jnp.log(jnp.float32(top)))


def draw_coupling(key, part):
    scales = row_scales(key, 3.0)
    key = jax.random.fold_in(key, 1)
    order = MB * NB
    factors = jax.random.randint(key, (order, 512), -2, 3)
    factors = factors.astype(jnp.float32)
    gram = jnp.dot(factors, factors.T, precision=lax.Precision.HIGHEST)
    outer = scales[:, None] * scales[None, :]
    matrix = gram * outer * jnp.float32(0.015625)
    return matrix.reshape(MB // N_PROW, N_PROW * NB, MB // N_PCOL, N_PCOL * NB)


def draw_diagonal(key, part):
    scales = row_scales(key, 3.0)
    key = jax.random.fold_in(key, 2)
    order = MB * NB
    level = jax.random.uniform(key, (order,), jnp.float32, 2.0, 8.0)
    shift = scales * scales * level
    return shift.reshape(MB // N_PROW, N_PROW * NB)


def setup_inputs(seed: int = 0) -> dict:
    seeds = jax.random.split(jax.random.key(seed), 3)
    coupling = draw_coupling(jax.random.fold_in(seeds[2], 71), 0)
    diagonal = draw_diagonal(jax.random.fold_in(seeds[2], 71), 0)
    return {"coupling": coupling, "diagonal": diagonal}


def factor_panel(column, diag_vector, start):
    pivot = column[start:start + NB] + jnp.diag(diag_vector[start:start + NB])
    lower_factor = jnp.linalg.cholesky(pivot)
    inverse = lax.linalg.triangular_solve(lower_factor, jnp.eye(NB, dtype=jnp.float32), left_side=True, lower=True)
    below = jnp.dot(column[start + NB:], inverse.T, precision=lax.Precision.HIGHEST)
    return jnp.concatenate([jnp.zeros((start, NB), jnp.float32), lower_factor, below], axis=0)

def reference(coupling, diagonal):
    order = MB * NB
    matrix = coupling.reshape(order, order)
    diag_vector = diagonal.reshape(order)
    first = factor_panel(matrix[:, :NB], diag_vector, 0)
    column = matrix[:, NB:2 * NB] - jnp.dot(first, first[NB:2 * NB].T, precision=lax.Precision.HIGHEST)
    second = factor_panel(column, diag_vector, NB)
    updated = matrix - jnp.dot(first, first.T, precision=lax.Precision.HIGHEST)
    updated = updated - jnp.dot(second, second.T, precision=lax.Precision.HIGHEST)
    position = jnp.arange(order)
    keeping = position >= 2 * NB
    updated = jnp.where(keeping[:, None] & keeping[None, :], updated, jnp.float32(0.0))
    return updated.reshape(coupling.shape)
```

```python
import functools
import math

import jax
import jax.numpy as jnp
from jax import lax
from jax.experimental import pallas as pl
from jax.experimental.pallas import tpu as pltpu
from jax.sharding import PartitionSpec as P

HIGHEST = lax.Precision.HIGHEST
MESH = pl.DeviceIdType.MESH
GROUP = 8
WINDOW = 4
PIECES = 4


def dot(a, b, contract):
    return lax.dot_general(
        a, b, (contract, ((), ())), precision=HIGHEST, preferred_element_type=jnp.float32
    )


def thirds(x):
    first = x.astype(jnp.bfloat16).astype(jnp.float32)
    rest = x - first
    second = rest.astype(jnp.bfloat16).astype(jnp.float32)
    return first, second, rest - second


def eliminate_group(work, group):
    size = work.shape[0]
    start = pl.multiple_of(group * GROUP, GROUP)
    lane = lax.broadcasted_iota(jnp.int32, (GROUP, size), 1) - start
    sub = lax.broadcasted_iota(jnp.int32, (GROUP, size), 0)
    rows = work[pl.ds(start, GROUP), :]
    cols = [
        jnp.broadcast_to(
            jnp.sum(jnp.where(lane == j, rows, 0.0), axis=1, keepdims=True), (GROUP, size)
        )
        for j in range(GROUP)
    ]
    own = (lane >= 0) & (lane < GROUP)
    rows = jnp.where(own, jnp.where(lane == sub, 1.0, 0.0), rows)
    for j in range(GROUP):
        scale = lax.rsqrt(cols[j][j:j + 1, :])
        row = rows[j:j + 1, :] * scale
        column = jnp.where(sub > j, cols[j] * scale, 0.0)
        rows = jnp.where(sub == j, row, rows - column * row)
        for m in range(j + 1, GROUP):
            cols[m] = cols[m] - column * (cols[m][j:j + 1, :] * scale)
    work[pl.ds(start, GROUP), :] = rows
    upper = jnp.where(lane >= GROUP, rows, 0.0)
    a1, a2, a3 = thirds(upper)
    b1, b2, b3 = thirds(rows)
    left = jnp.concatenate([a1, a1, a2, a2, a1, a3], axis=0).astype(jnp.bfloat16)
    right = jnp.concatenate([b1, b2, b1, b2, b3, b1], axis=0).astype(jnp.bfloat16)
    product = lax.dot_general(
        left, right, (((0,), (0,)), ((), ())), preferred_element_type=jnp.float32
    )
    lane_all = lax.broadcasted_iota(jnp.int32, (size, size), 1) - start
    row_all = lax.broadcasted_iota(jnp.int32, (size, size), 0) - start
    dead = (row_all >= GROUP) & (lane_all >= 0) & (lane_all < GROUP)
    work[...] = jnp.where(dead, 0.0, work[...]) - product


def lower_part(x):
    size = x.shape[0]
    row = lax.broadcasted_iota(jnp.int32, (size, size), 0)
    col = lax.broadcasted_iota(jnp.int32, (size, size), 1)
    return jnp.where(row >= col, x, 0.0)


def with_diagonal(block, shift_row):
    size = block.shape[0]
    row = lax.broadcasted_iota(jnp.int32, (size, size), 0)
    col = lax.broadcasted_iota(jnp.int32, (size, size), 1)
    return jnp.where(row == col, block + shift_row, block)


def share_kernel(
    n_prow, n_pcol, width, column, coupling, own_shift, panel, across, pivots, shift,
    local_sem, next_send, next_recv, mate_send, mate_recv,
    pivot_send, pivot_recv, pivot_local, cross_send, cross_recv, shift_send, shift_recv,
):
    p = lax.axis_index("prow")
    q = lax.axis_index("pcol")
    chunks = column.shape[0]
    block = coupling.shape[1]
    height = n_prow // width
    side = q % 2
    mate = q + 1 - 2 * side
    other = 1 - side
    y = p // width
    x = p % width

    barrier = pltpu.get_barrier_semaphore()
    for d in range(1, n_prow):
        pl.semaphore_signal(
            barrier, inc=1, device_id={"prow": (p + d) % n_prow}, device_id_type=MESH
        )
    pl.semaphore_signal(barrier, inc=1, device_id={"pcol": mate}, device_id_type=MESH)

    @pl.when(q >= 2)
    def _():
        pl.semaphore_signal(barrier, inc=1, device_id={"pcol": q - 2}, device_id_type=MESH)

    @pl.when(q + 2 < n_pcol)
    def _():
        pl.semaphore_signal(barrier, inc=1, device_id={"pcol": q + 2}, device_id_type=MESH)

    own_column = pltpu.make_async_copy(column, panel.at[side], local_sem.at[0])
    own_across = pltpu.make_async_copy(coupling.at[0], across.at[p % 2], local_sem.at[1])

    @pl.when(q < 2)
    def _():
        own_column.start()

    @pl.when(p < 2)
    def _():
        own_across.start()

    @pl.when(q < 2)
    def _():
        own_column.wait()

    @pl.when(p < 2)
    def _():
        own_across.wait()

    pl.semaphore_wait(
        barrier,
        n_prow + jnp.where(q >= 2, 1, 0) + jnp.where(q + 2 < n_pcol, 1, 0),
    )

    def to_next(k):
        return pltpu.make_async_remote_copy(
            src_ref=panel.at[side, k], dst_ref=panel.at[side, k],
            send_sem=next_send.at[k], recv_sem=next_recv.at[k],
            device_id={"pcol": jnp.minimum(q + 2, n_pcol - 2 + side)}, device_id_type=MESH,
        )

    def to_mate(k):
        return pltpu.make_async_remote_copy(
            src_ref=panel.at[side, k], dst_ref=panel.at[side, k],
            send_sem=mate_send.at[k], recv_sem=mate_recv.at[k],
            device_id={"pcol": mate}, device_id_type=MESH,
        )

    def from_mate(k):
        return pltpu.make_async_remote_copy(
            src_ref=panel.at[other, k], dst_ref=panel.at[other, k],
            send_sem=mate_send.at[k], recv_sem=mate_recv.at[k],
            device_id={"pcol": mate}, device_id_type=MESH,
        )

    def forward(k):
        @pl.when(q >= 2)
        def _():
            to_next(k).wait_recv()

        @pl.when(q + 2 < n_pcol)
        def _():
            to_next(k).start()

        to_mate(k).start()

    def sent(k):
        @pl.when(q + 2 < n_pcol)
        def _():
            to_next(k).wait_send()

        to_mate(k).wait_send()

    def pivot_copy(i, d, source):
        return pltpu.make_async_remote_copy(
            src_ref=panel.at[source, 0], dst_ref=pivots.at[i],
            send_sem=pivot_send.at[i, d], recv_sem=pivot_recv.at[i],
            device_id={"prow": (p + d) % n_prow}, device_id_type=MESH,
        )

    parts = ((0, 0, 0), (1, 1, 0), (2, 1, 1))

    def shift_copy(i, d):
        return pltpu.make_async_remote_copy(
            src_ref=own_shift, dst_ref=shift.at[i],
            send_sem=shift_send.at[i, d], recv_sem=shift_recv.at[i],
            device_id={"prow": (p + d) % n_prow}, device_id_type=MESH,
        )

    def shift_local(i):
        return pltpu.make_async_copy(own_shift, shift.at[i], local_sem.at[2 + i])

    def cross_copy(s, piece, way):
        rows = block // PIECES
        part = across.at[s, pl.ds(piece * rows, rows)]
        step = (width, 1, -1)[way]
        return pltpu.make_async_remote_copy(
            src_ref=part, dst_ref=part,
            send_sem=cross_send.at[s, piece, way], recv_sem=cross_recv.at[s, piece],
            device_id={"prow": (p + step + n_prow) % n_prow}, device_id_type=MESH,
        )

    def ways(s):
        return (
            (x == s) & (y + 1 < height),
            (x >= s) & (x + 1 < width),
            (x <= s) & (x >= 1),
        )

    def cross(piece):
        for s in (0, 1):
            @pl.when(p != s)
            def _():
                cross_copy(s, piece, 0).wait_recv()

            for way, goes in enumerate(ways(s)):
                @pl.when(goes)
                def _():
                    cross_copy(s, piece, way).start()

    forward(0)
    for i in (0, 1):
        @pl.when(p == i)
        def _():
            for d in range(1, n_prow):
                shift_copy(i, d).start()
            shift_local(i).start()

    from_mate(0).wait_recv()
    for i, owner, source in parts:
        @pl.when(p == owner)
        def _():
            for d in range(1, n_prow):
                pivot_copy(i, d, source).start()
            pltpu.make_async_copy(panel.at[source, 0], pivots.at[i], pivot_local.at[i]).start()

    @pl.loop(1, chunks)
    def _(k):
        forward(k)

        @pl.when(k <= PIECES)
        def _():
            cross(k - 1)

        @pl.when(k >= WINDOW)
        def _():
            sent(k - WINDOW)

    for i, owner, source in parts:
        @pl.when(p == owner)
        def _():
            for d in range(1, n_prow):
                pivot_copy(i, d, source).wait_send()
            pltpu.make_async_copy(panel.at[source, 0], pivots.at[i], pivot_local.at[i]).wait()

        @pl.when(p != owner)
        def _():
            pivot_copy(i, 1, source).wait_recv()

    for i in (0, 1):
        @pl.when(p == i)
        def _():
            for d in range(1, n_prow):
                shift_copy(i, d).wait_send()
            shift_local(i).wait()

        @pl.when(p != i)
        def _():
            shift_copy(i, 1).wait_recv()

    @pl.loop(0, PIECES)
    def _(piece):
        for s in (0, 1):
            for way, goes in enumerate(ways(s)):
                @pl.when(goes)
                def _():
                    cross_copy(s, piece, way).wait_send()

    @pl.loop(chunks - WINDOW, chunks)
    def _(k):
        sent(k)

    @pl.loop(1, chunks)
    def _(k):
        from_mate(k).wait_recv()


def update_kernel(
    n_prow, n_pcol, matrix, panel, across, pivots, shift, out, work, inverse, below, right
):
    step = pl.program_id(0)
    size = panel.shape[-1]
    col_blocks = matrix.shape[1] // size

    @pl.when(step == 0)
    def _():
        def factor(i):
            @pl.loop(0, size // GROUP)
            def _(group):
                eliminate_group(work, group)

            inverse[i] = lower_part(work[...])

        work[...] = with_diagonal(pivots[0], shift[0, 0:1, :])
        factor(0)
        below[...] = dot(pivots[1], inverse[0], ((1,), (1,)))
        work[...] = with_diagonal(pivots[2], shift[1, 0:1, :]) - dot(
            below[...], below[...], ((1,), (1,))
        )
        factor(1)
        for c in range(col_blocks):
            lanes = slice(c * size, (c + 1) * size)
            first = dot(inverse[0], across[0, pl.ds(c, size, stride=col_blocks), :], ((1,), (0,)))
            second = across[1, pl.ds(c, size, stride=col_blocks), :] - dot(
                below[...], first, ((1,), (0,))
            )
            second = dot(inverse[1], second, ((1,), (0,)))
            for i, part in enumerate((first, second)):
                high = part.astype(jnp.bfloat16)
                low = (part - high.astype(jnp.float32)).astype(jnp.bfloat16)
                for j, piece in enumerate((high, low, high)):
                    right[(2 * j + i) * size:(2 * j + i + 1) * size, lanes] = piece

    first = dot(panel[0, 0], inverse[0], ((1,), (1,)))
    second = panel[1, 0] - dot(first, below[...], ((1,), (1,)))
    second = dot(second, inverse[1], ((1,), (1,)))
    left = jnp.concatenate([first, second], axis=1)
    high = left.astype(jnp.bfloat16)
    low = (left - high.astype(jnp.float32)).astype(jnp.bfloat16)
    left = jnp.concatenate([high, high, low], axis=1)
    product = jnp.dot(left, right[...], preferred_element_type=jnp.float32)
    row_kept = step * n_prow + lax.axis_index("prow") >= 2
    q = lax.axis_index("pcol")
    for c in range(col_blocks):
        rows = pl.ds(c, size, stride=col_blocks)
        kept = row_kept & (c * n_pcol + q >= 2)
        value = matrix[0, rows, :] - product[:, c * size:(c + 1) * size]
        out[0, rows, :] = jnp.where(kept, value, 0.0)


def on_device(n_prow, n_pcol, coupling, diagonal):
    chunks, size, col_blocks, _ = coupling.shape
    root = math.isqrt(n_prow)
    width = root if root * root == n_prow else n_prow
    f32 = jnp.float32
    dma = pltpu.SemaphoreType.DMA
    column = coupling[:, :, 0, :]
    own_shift = jnp.broadcast_to(diagonal[0], (8, size))
    panel, across, pivots, shift = pl.pallas_call(
        functools.partial(share_kernel, n_prow, n_pcol, width),
        out_shape=(
            jax.ShapeDtypeStruct((2, chunks, size, size), f32),
            jax.ShapeDtypeStruct((2, size, col_blocks, size), f32),
            jax.ShapeDtypeStruct((3, size, size), f32),
            jax.ShapeDtypeStruct((2, 8, size), f32),
        ),
        in_specs=[pl.BlockSpec(memory_space=pl.ANY)] * 3,
        out_specs=(pl.BlockSpec(memory_space=pl.ANY),) * 4,
        scratch_shapes=[
            dma((4,)), dma((chunks,)), dma((chunks,)), dma((chunks,)), dma((chunks,)),
            dma((3, n_prow)), dma((3,)), dma((3,)),
            dma((2, PIECES, 3)), dma((2, PIECES)), dma((2, n_prow)), dma((2,)),
        ],
        compiler_params=pltpu.CompilerParams(collective_id=0, has_side_effects=True),
        name="share_panels",
    )(column, coupling, own_shift)
    out = pl.pallas_call(
        functools.partial(update_kernel, n_prow, n_pcol),
        grid=(chunks,),
        out_shape=jax.ShapeDtypeStruct((chunks, size * col_blocks, size), f32),
        in_specs=[
            pl.BlockSpec((1, size * col_blocks, size), lambda i: (i, 0, 0)),
            pl.BlockSpec((2, 1, size, size), lambda i: (0, i, 0, 0)),
            pl.BlockSpec((2, size * col_blocks, size), lambda i: (0, 0, 0)),
            pl.BlockSpec((3, size, size), lambda i: (0, 0, 0)),
            pl.BlockSpec((2, 8, size), lambda i: (0, 0, 0)),
        ],
        out_specs=pl.BlockSpec((1, size * col_blocks, size), lambda i: (i, 0, 0)),
        scratch_shapes=[
            pltpu.VMEM((size, size), f32),
            pltpu.VMEM((2, size, size), f32),
            pltpu.VMEM((size, size), f32),
            pltpu.VMEM((6 * size, col_blocks * size), jnp.bfloat16),
        ],
        compiler_params=pltpu.CompilerParams(vmem_limit_bytes=40 * 1024 * 1024),
        name="update_trailing",
    )(
        coupling.reshape(chunks, size * col_blocks, size),
        panel,
        across.reshape(2, size * col_blocks, size),
        pivots,
        shift,
    )
    return out.reshape(coupling.shape)


def solution(mesh):
    return jax.shard_map(
        functools.partial(on_device, mesh.shape["prow"], mesh.shape["pcol"]),
        mesh=mesh,
        in_specs=(P(None, "prow", None, "pcol"), P(None, "prow")),
        out_specs=P(None, "prow", None, "pcol"),
        check_vma=False,
    )
```

```python
import functools
import math

import jax
import jax.numpy as jnp
from jax import lax
from jax.experimental import pallas as pl
from jax.experimental.pallas import tpu as pltpu
from jax.sharding import PartitionSpec as P

HIGHEST = lax.Precision.HIGHEST
MESH = pl.DeviceIdType.MESH
GROUP = 8
PIECES = 4


def dot(a, b, contract):
    return lax.dot_general(
        a, b, (contract, ((), ())), precision=HIGHEST, preferred_element_type=jnp.float32
    )


def thirds(x):
    first = x.astype(jnp.bfloat16).astype(jnp.float32)
    rest = x - first
    second = rest.astype(jnp.bfloat16).astype(jnp.float32)
    return first, second, rest - second


def eliminate_group(work, group):
    size = work.shape[0]
    start = pl.multiple_of(group * GROUP, GROUP)
    lane = lax.broadcasted_iota(jnp.int32, (GROUP, size), 1) - start
    sub = lax.broadcasted_iota(jnp.int32, (GROUP, size), 0)
    rows = work[pl.ds(start, GROUP), :]
    cols = [
        jnp.broadcast_to(
            jnp.sum(jnp.where(lane == j, rows, 0.0), axis=1, keepdims=True), (GROUP, size)
        )
        for j in range(GROUP)
    ]
    own = (lane >= 0) & (lane < GROUP)
    rows = jnp.where(own, jnp.where(lane == sub, 1.0, 0.0), rows)
    for j in range(GROUP):
        scale = lax.rsqrt(cols[j][j:j + 1, :])
        row = rows[j:j + 1, :] * scale
        column = jnp.where(sub > j, cols[j] * scale, 0.0)
        rows = jnp.where(sub == j, row, rows - column * row)
        for m in range(j + 1, GROUP):
            cols[m] = cols[m] - column * (cols[m][j:j + 1, :] * scale)
    work[pl.ds(start, GROUP), :] = rows
    upper = jnp.where(lane >= GROUP, rows, 0.0)
    a1, a2, a3 = thirds(upper)
    b1, b2, b3 = thirds(rows)
    left = jnp.concatenate([a1, a1, a2, a2, a1, a3], axis=0).astype(jnp.bfloat16)
    right = jnp.concatenate([b1, b2, b1, b2, b3, b1], axis=0).astype(jnp.bfloat16)
    product = lax.dot_general(
        left, right, (((0,), (0,)), ((), ())), preferred_element_type=jnp.float32
    )
    lane_all = lax.broadcasted_iota(jnp.int32, (size, size), 1) - start
    row_all = lax.broadcasted_iota(jnp.int32, (size, size), 0) - start
    dead = (row_all >= GROUP) & (lane_all >= 0) & (lane_all < GROUP)
    work[...] = jnp.where(dead, 0.0, work[...]) - product


def lower_part(x):
    size = x.shape[0]
    row = lax.broadcasted_iota(jnp.int32, (size, size), 0)
    col = lax.broadcasted_iota(jnp.int32, (size, size), 1)
    return jnp.where(row >= col, x, 0.0)


def with_diagonal(block, shift_row):
    size = block.shape[0]
    row = lax.broadcasted_iota(jnp.int32, (size, size), 0)
    col = lax.broadcasted_iota(jnp.int32, (size, size), 1)
    return jnp.where(row == col, block + shift_row, block)


def share_kernel(
    n_prow, n_pcol, width, coupling, own_shift, panel, across, inverse, below,
    pivots, shift, work, local_sem, next_send, next_recv, mate_send, mate_recv,
    pivot_send, pivot_recv, pivot_local, cross_send, cross_recv, shift_send, shift_recv,
):
    p = lax.axis_index("prow")
    q = lax.axis_index("pcol")
    chunks, block = coupling.shape[:2]
    height = n_prow // width
    side = q % 2
    mate = q + 1 - 2 * side
    other = 1 - side
    y = p // width
    x = p % width

    barrier = pltpu.get_barrier_semaphore()
    for d in range(1, n_prow):
        pl.semaphore_signal(
            barrier, inc=1, device_id={"prow": (p + d) % n_prow}, device_id_type=MESH
        )
    pl.semaphore_signal(barrier, inc=1, device_id={"pcol": mate}, device_id_type=MESH)

    @pl.when(q >= 2)
    def _():
        pl.semaphore_signal(barrier, inc=1, device_id={"pcol": q - 2}, device_id_type=MESH)

    @pl.when(q + 2 < n_pcol)
    def _():
        pl.semaphore_signal(barrier, inc=1, device_id={"pcol": q + 2}, device_id_type=MESH)

    own_column = pltpu.make_async_copy(
        coupling.at[:, :, 0, :], panel.at[side], local_sem.at[0]
    )
    own_across = pltpu.make_async_copy(coupling.at[0], across.at[p % 2], local_sem.at[1])

    @pl.when(q < 2)
    def _():
        own_column.start()

    @pl.when(p < 2)
    def _():
        own_across.start()

    @pl.when(q < 2)
    def _():
        own_column.wait()

    @pl.when(p < 2)
    def _():
        own_across.wait()

    pl.semaphore_wait(
        barrier,
        n_prow + jnp.where(q >= 2, 1, 0) + jnp.where(q + 2 < n_pcol, 1, 0),
    )

    def to_next(k):
        return pltpu.make_async_remote_copy(
            src_ref=panel.at[side, k], dst_ref=panel.at[side, k],
            send_sem=next_send.at[k], recv_sem=next_recv.at[k],
            device_id={"pcol": jnp.minimum(q + 2, n_pcol - 2 + side)}, device_id_type=MESH,
        )

    def to_mate(k):
        return pltpu.make_async_remote_copy(
            src_ref=panel.at[side, k], dst_ref=panel.at[side, k],
            send_sem=mate_send.at[k], recv_sem=mate_recv.at[k],
            device_id={"pcol": mate}, device_id_type=MESH,
        )

    def from_mate(k):
        return pltpu.make_async_remote_copy(
            src_ref=panel.at[other, k], dst_ref=panel.at[other, k],
            send_sem=mate_send.at[k], recv_sem=mate_recv.at[k],
            device_id={"pcol": mate}, device_id_type=MESH,
        )

    def forward(k):
        @pl.when(q >= 2)
        def _():
            to_next(k).wait_recv()

        @pl.when(q + 2 < n_pcol)
        def _():
            to_next(k).start()

        to_mate(k).start()

    def sent(k):
        @pl.when(q + 2 < n_pcol)
        def _():
            to_next(k).wait_send()

        to_mate(k).wait_send()

    def pivot_copy(i, d, source):
        return pltpu.make_async_remote_copy(
            src_ref=panel.at[source, 0], dst_ref=pivots.at[i],
            send_sem=pivot_send.at[i, d], recv_sem=pivot_recv.at[i],
            device_id={"prow": (p + d) % n_prow}, device_id_type=MESH,
        )

    parts = ((0, 0, 0), (1, 1, 0), (2, 1, 1))

    def shift_copy(i, d):
        return pltpu.make_async_remote_copy(
            src_ref=own_shift, dst_ref=shift.at[i],
            send_sem=shift_send.at[i, d], recv_sem=shift_recv.at[i],
            device_id={"prow": (p + d) % n_prow}, device_id_type=MESH,
        )

    def shift_local(i):
        return pltpu.make_async_copy(own_shift, shift.at[i], local_sem.at[2 + i])

    def cross_copy(s, piece, way):
        rows = block // PIECES
        part = across.at[s, pl.ds(piece * rows, rows)]
        step = (width, 1, -1)[way]
        return pltpu.make_async_remote_copy(
            src_ref=part, dst_ref=part,
            send_sem=cross_send.at[s, piece, way], recv_sem=cross_recv.at[s, piece],
            device_id={"prow": (p + step + n_prow) % n_prow}, device_id_type=MESH,
        )

    def ways(s):
        return (
            (x == s) & (y + 1 < height),
            (x >= s) & (x + 1 < width),
            (x <= s) & (x >= 1),
        )

    def cross(piece):
        for s in (0, 1):
            @pl.when(p != s)
            def _():
                cross_copy(s, piece, 0).wait_recv()

            for way, goes in enumerate(ways(s)):
                @pl.when(goes)
                def _():
                    cross_copy(s, piece, way).start()

    forward(0)
    for i in (0, 1):
        @pl.when(p == i)
        def _():
            for d in range(1, n_prow):
                shift_copy(i, d).start()
            shift_local(i).start()

    from_mate(0).wait_recv()
    for i, owner, source in parts:
        @pl.when(p == owner)
        def _():
            for d in range(1, n_prow):
                pivot_copy(i, d, source).start()
            pltpu.make_async_copy(panel.at[source, 0], pivots.at[i], pivot_local.at[i]).start()

    forward(1)
    forward(2)

    def arrived(i, owner, source):
        @pl.when(p == owner)
        def _():
            pltpu.make_async_copy(panel.at[source, 0], pivots.at[i], pivot_local.at[i]).wait()

        @pl.when(p != owner)
        def _():
            pivot_copy(i, 1, source).wait_recv()

    def shift_arrived(i):
        @pl.when(p == i)
        def _():
            shift_local(i).wait()

        @pl.when(p != i)
        def _():
            shift_copy(i, 1).wait_recv()

    def pass_on(slot):
        k = slot + 3

        @pl.when(k < chunks)
        def _():
            forward(k)
            sent(k - 3)

        @pl.when(slot < PIECES)
        def _():
            cross(slot)

    slots = block // (2 * GROUP)

    def factor(i):
        @pl.loop(0, slots)
        def _(slot):
            pass_on(i * slots + slot)
            eliminate_group(work, 2 * slot)
            eliminate_group(work, 2 * slot + 1)

        inverse[i] = lower_part(work[...])

    shift_arrived(0)
    arrived(*parts[0])
    work[...] = with_diagonal(pivots[0], shift[0, 0:1, :])
    factor(0)
    shift_arrived(1)
    arrived(*parts[1])
    arrived(*parts[2])
    below[...] = dot(pivots[1], inverse[0], ((1,), (1,)))
    work[...] = with_diagonal(pivots[2], shift[1, 0:1, :]) - dot(
        below[...], below[...], ((1,), (1,))
    )
    factor(1)

    @pl.loop(2 * slots, max(chunks - 3, 2 * slots))
    def _(slot):
        pass_on(slot)

    for i, owner, source in parts:
        @pl.when(p == owner)
        def _():
            for d in range(1, n_prow):
                pivot_copy(i, d, source).wait_send()

    for i in (0, 1):
        @pl.when(p == i)
        def _():
            for d in range(1, n_prow):
                shift_copy(i, d).wait_send()

    @pl.loop(0, PIECES)
    def _(piece):
        for s in (0, 1):
            for way, goes in enumerate(ways(s)):
                @pl.when(goes)
                def _():
                    cross_copy(s, piece, way).wait_send()

    @pl.loop(chunks - 3, chunks)
    def _(k):
        sent(k)

    @pl.loop(1, chunks)
    def _(k):
        from_mate(k).wait_recv()


def update_kernel(
    n_prow, n_pcol, matrix, panel, across, inverse, below, out, right
):
    step = pl.program_id(0)
    size = panel.shape[-1]
    col_blocks = matrix.shape[1] // size

    @pl.when(step == 0)
    def _():
        for c in range(col_blocks):
            lanes = slice(c * size, (c + 1) * size)
            first = dot(inverse[0], across[0, pl.ds(c, size, stride=col_blocks), :], ((1,), (0,)))
            second = across[1, pl.ds(c, size, stride=col_blocks), :] - dot(
                below[...], first, ((1,), (0,))
            )
            second = dot(inverse[1], second, ((1,), (0,)))
            for i, part in enumerate((first, second)):
                high = part.astype(jnp.bfloat16)
                low = (part - high.astype(jnp.float32)).astype(jnp.bfloat16)
                for j, piece in enumerate((high, low, high)):
                    right[(2 * j + i) * size:(2 * j + i + 1) * size, lanes] = piece

    first = dot(panel[0, 0], inverse[0], ((1,), (1,)))
    second = panel[1, 0] - dot(first, below[...], ((1,), (1,)))
    second = dot(second, inverse[1], ((1,), (1,)))
    left = jnp.concatenate([first, second], axis=1)
    high = left.astype(jnp.bfloat16)
    low = (left - high.astype(jnp.float32)).astype(jnp.bfloat16)
    left = jnp.concatenate([high, high, low], axis=1)
    product = jnp.dot(left, right[...], preferred_element_type=jnp.float32)
    row_kept = step * n_prow + lax.axis_index("prow") >= 2
    q = lax.axis_index("pcol")
    for c in range(col_blocks):
        rows = pl.ds(c, size, stride=col_blocks)
        kept = row_kept & (c * n_pcol + q >= 2)
        value = matrix[0, rows, :] - product[:, c * size:(c + 1) * size]
        out[0, rows, :] = jnp.where(kept, value, 0.0)


def on_device(n_prow, n_pcol, coupling, diagonal):
    chunks, size, col_blocks, _ = coupling.shape
    root = math.isqrt(n_prow)
    width = root if root * root == n_prow else n_prow
    f32 = jnp.float32
    dma = pltpu.SemaphoreType.DMA
    vmem = pl.BlockSpec(memory_space=pltpu.VMEM)
    own_shift = jnp.broadcast_to(diagonal[0], (8, size))
    panel, across, inverse, below = pl.pallas_call(
        functools.partial(share_kernel, n_prow, n_pcol, width),
        out_shape=(
            jax.ShapeDtypeStruct((2, chunks, size, size), f32),
            jax.ShapeDtypeStruct((2, size, col_blocks, size), f32),
            jax.ShapeDtypeStruct((2, size, size), f32),
            jax.ShapeDtypeStruct((size, size), f32),
        ),
        in_specs=[pl.BlockSpec(memory_space=pl.ANY), vmem],
        out_specs=(vmem,) * 4,
        scratch_shapes=[
            pltpu.VMEM((3, size, size), f32),
            pltpu.VMEM((2, 8, size), f32),
            pltpu.VMEM((size, size), f32),
            dma((4,)), dma((chunks,)), dma((chunks,)), dma((chunks,)), dma((chunks,)),
            dma((3, n_prow)), dma((3,)), dma((3,)),
            dma((2, PIECES, 3)), dma((2, PIECES)), dma((2, n_prow)), dma((2,)),
        ],
        compiler_params=pltpu.CompilerParams(
            collective_id=0, has_side_effects=True, vmem_limit_bytes=60 * 1024 * 1024
        ),
        name="share_panels",
    )(coupling, own_shift)
    out = pl.pallas_call(
        functools.partial(update_kernel, n_prow, n_pcol),
        grid=(chunks,),
        out_shape=jax.ShapeDtypeStruct((chunks, size * col_blocks, size), f32),
        in_specs=[
            pl.BlockSpec((1, size * col_blocks, size), lambda i: (i, 0, 0)),
            pl.BlockSpec((2, 1, size, size), lambda i: (0, i, 0, 0)),
            pl.BlockSpec((2, size * col_blocks, size), lambda i: (0, 0, 0)),
            pl.BlockSpec((2, size, size), lambda i: (0, 0, 0)),
            pl.BlockSpec((size, size), lambda i: (0, 0)),
        ],
        out_specs=pl.BlockSpec((1, size * col_blocks, size), lambda i: (i, 0, 0)),
        scratch_shapes=[
            pltpu.VMEM((6 * size, col_blocks * size), jnp.bfloat16),
        ],
        compiler_params=pltpu.CompilerParams(vmem_limit_bytes=60 * 1024 * 1024),
        name="update_trailing",
    )(
        coupling.reshape(chunks, size * col_blocks, size),
        panel,
        across.reshape(2, size * col_blocks, size),
        inverse,
        below,
    )
    return out.reshape(coupling.shape)


def solution(mesh):
    return jax.shard_map(
        functools.partial(on_device, mesh.shape["prow"], mesh.shape["pcol"]),
        mesh=mesh,
        in_specs=(P(None, "prow", None, "pcol"), P(None, "prow")),
        out_specs=P(None, "prow", None, "pcol"),
        check_vma=False,
    )
```

```python
import functools
import math

import jax
import jax.numpy as jnp
from jax import lax
from jax.experimental import pallas as pl
from jax.experimental.pallas import tpu as pltpu
from jax.sharding import PartitionSpec as P

HIGHEST = lax.Precision.HIGHEST
MESH = pl.DeviceIdType.MESH
GROUP = 8
PIECES = 4


def dot(a, b, contract):
    return lax.dot_general(
        a, b, (contract, ((), ())), precision=HIGHEST, preferred_element_type=jnp.float32
    )


def thirds(x):
    first = x.astype(jnp.bfloat16).astype(jnp.float32)
    rest = x - first
    second = rest.astype(jnp.bfloat16).astype(jnp.float32)
    return first, second, rest - second


def eliminate_group(work, group):
    size = work.shape[0]
    start = pl.multiple_of(group * GROUP, GROUP)
    lane = lax.broadcasted_iota(jnp.int32, (GROUP, size), 1) - start
    sub = lax.broadcasted_iota(jnp.int32, (GROUP, size), 0)
    rows = work[pl.ds(start, GROUP), :]
    cols = [
        jnp.broadcast_to(
            jnp.sum(jnp.where(lane == j, rows, 0.0), axis=1, keepdims=True), (GROUP, size)
        )
        for j in range(GROUP)
    ]
    own = (lane >= 0) & (lane < GROUP)
    rows = jnp.where(own, jnp.where(lane == sub, 1.0, 0.0), rows)
    for j in range(GROUP):
        scale = lax.rsqrt(cols[j][j:j + 1, :])
        row = rows[j:j + 1, :] * scale
        column = jnp.where(sub > j, cols[j] * scale, 0.0)
        rows = jnp.where(sub == j, row, rows - column * row)
        for m in range(j + 1, GROUP):
            cols[m] = cols[m] - column * (cols[m][j:j + 1, :] * scale)
    work[pl.ds(start, GROUP), :] = rows
    upper = jnp.where(lane >= GROUP, rows, 0.0)
    a1, a2, a3 = thirds(upper)
    b1, b2, b3 = thirds(rows)
    left = jnp.concatenate([a1, a1, a2, a2, a1, a3], axis=0).astype(jnp.bfloat16)
    right = jnp.concatenate([b1, b2, b1, b2, b3, b1], axis=0).astype(jnp.bfloat16)
    product = lax.dot_general(
        left, right, (((0,), (0,)), ((), ())), preferred_element_type=jnp.float32
    )
    lane_all = lax.broadcasted_iota(jnp.int32, (size, size), 1) - start
    row_all = lax.broadcasted_iota(jnp.int32, (size, size), 0) - start
    dead = (row_all >= GROUP) & (lane_all >= 0) & (lane_all < GROUP)
    work[...] = jnp.where(dead, 0.0, work[...]) - product


def lower_part(x):
    size = x.shape[0]
    row = lax.broadcasted_iota(jnp.int32, (size, size), 0)
    col = lax.broadcasted_iota(jnp.int32, (size, size), 1)
    return jnp.where(row >= col, x, 0.0)


def with_diagonal(block, shift_row):
    size = block.shape[0]
    row = lax.broadcasted_iota(jnp.int32, (size, size), 0)
    col = lax.broadcasted_iota(jnp.int32, (size, size), 1)
    return jnp.where(row == col, block + shift_row, block)


def share_kernel(
    n_prow, n_pcol, width, coupling, own_shift, panel, across, inverse,
    pivots, shift, work, below, stage, stage_sem, local_sem, next_send, next_recv, mate_send, mate_recv,
    pivot_send, pivot_recv, pivot_local, cross_send, cross_recv, shift_send, shift_recv,
):
    p = lax.axis_index("prow")
    q = lax.axis_index("pcol")
    chunks, block = coupling.shape[:2]
    height = n_prow // width
    side = q % 2
    mate = q + 1 - 2 * side
    other = 1 - side
    y = p // width
    x = p % width

    barrier = pltpu.get_barrier_semaphore()
    for d in range(1, n_prow):
        pl.semaphore_signal(
            barrier, inc=1, device_id={"prow": (p + d) % n_prow}, device_id_type=MESH
        )
    pl.semaphore_signal(barrier, inc=1, device_id={"pcol": mate}, device_id_type=MESH)

    @pl.when(q >= 2)
    def _():
        pl.semaphore_signal(barrier, inc=1, device_id={"pcol": q - 2}, device_id_type=MESH)

    @pl.when(q + 2 < n_pcol)
    def _():
        pl.semaphore_signal(barrier, inc=1, device_id={"pcol": q + 2}, device_id_type=MESH)

    def staged(k):
        return pltpu.make_async_copy(coupling.at[k], stage.at[k], stage_sem.at[k])

    own_across = pltpu.make_async_copy(coupling.at[0], across.at[p % 2], local_sem.at[1])

    @pl.when(q < 2)
    def _():
        @pl.loop(0, chunks)
        def _(k):
            staged(k).start()

    @pl.when(p < 2)
    def _():
        own_across.start()

    @pl.when(p < 2)
    def _():
        own_across.wait()

    pl.semaphore_wait(
        barrier,
        n_prow + jnp.where(q >= 2, 1, 0) + jnp.where(q + 2 < n_pcol, 1, 0),
    )

    def to_next(k):
        return pltpu.make_async_remote_copy(
            src_ref=panel.at[side, k], dst_ref=panel.at[side, k],
            send_sem=next_send.at[k], recv_sem=next_recv.at[k],
            device_id={"pcol": jnp.minimum(q + 2, n_pcol - 2 + side)}, device_id_type=MESH,
        )

    def to_mate(k):
        return pltpu.make_async_remote_copy(
            src_ref=panel.at[side, k], dst_ref=panel.at[side, k],
            send_sem=mate_send.at[k], recv_sem=mate_recv.at[k],
            device_id={"pcol": mate}, device_id_type=MESH,
        )

    def from_mate(k):
        return pltpu.make_async_remote_copy(
            src_ref=panel.at[other, k], dst_ref=panel.at[other, k],
            send_sem=mate_send.at[k], recv_sem=mate_recv.at[k],
            device_id={"pcol": mate}, device_id_type=MESH,
        )

    def forward(k):
        @pl.when(q < 2)
        def _():
            staged(k).wait()
            panel[side, k] = stage[k, :, 0, :]

        @pl.when(q >= 2)
        def _():
            to_next(k).wait_recv()

        @pl.when(q + 2 < n_pcol)
        def _():
            to_next(k).start()

        to_mate(k).start()

    def sent(k):
        @pl.when(q + 2 < n_pcol)
        def _():
            to_next(k).wait_send()

        to_mate(k).wait_send()

    def pivot_copy(i, d, source):
        return pltpu.make_async_remote_copy(
            src_ref=panel.at[source, 0], dst_ref=pivots.at[i],
            send_sem=pivot_send.at[i, d], recv_sem=pivot_recv.at[i],
            device_id={"prow": (p + d) % n_prow}, device_id_type=MESH,
        )

    parts = ((0, 0, 0), (1, 1, 0), (2, 1, 1))

    def shift_copy(i, d):
        return pltpu.make_async_remote_copy(
            src_ref=own_shift, dst_ref=shift.at[i],
            send_sem=shift_send.at[i, d], recv_sem=shift_recv.at[i],
            device_id={"prow": (p + d) % n_prow}, device_id_type=MESH,
        )

    def shift_local(i):
        return pltpu.make_async_copy(own_shift, shift.at[i], local_sem.at[2 + i])

    def cross_copy(s, piece, way):
        rows = block // PIECES
        part = across.at[s, pl.ds(piece * rows, rows)]
        step = (width, 1, -1)[way]
        return pltpu.make_async_remote_copy(
            src_ref=part, dst_ref=part,
            send_sem=cross_send.at[s, piece, way], recv_sem=cross_recv.at[s, piece],
            device_id={"prow": (p + step + n_prow) % n_prow}, device_id_type=MESH,
        )

    def ways(s):
        return (
            (x == s) & (y + 1 < height),
            (x >= s) & (x + 1 < width),
            (x <= s) & (x >= 1),
        )

    def cross(piece):
        for s in (0, 1):
            @pl.when(p != s)
            def _():
                cross_copy(s, piece, 0).wait_recv()

            for way, goes in enumerate(ways(s)):
                @pl.when(goes)
                def _():
                    cross_copy(s, piece, way).start()

    forward(0)
    for i in (0, 1):
        @pl.when(p == i)
        def _():
            for d in range(1, n_prow):
                shift_copy(i, d).start()
            shift_local(i).start()

    from_mate(0).wait_recv()
    for i, owner, source in parts:
        @pl.when(p == owner)
        def _():
            for d in range(1, n_prow):
                pivot_copy(i, d, source).start()
            pltpu.make_async_copy(panel.at[source, 0], pivots.at[i], pivot_local.at[i]).start()

    forward(1)
    forward(2)

    def arrived(i, owner, source):
        @pl.when(p == owner)
        def _():
            pltpu.make_async_copy(panel.at[source, 0], pivots.at[i], pivot_local.at[i]).wait()

        @pl.when(p != owner)
        def _():
            pivot_copy(i, 1, source).wait_recv()

    def shift_arrived(i):
        @pl.when(p == i)
        def _():
            shift_local(i).wait()

        @pl.when(p != i)
        def _():
            shift_copy(i, 1).wait_recv()

    def pass_on(slot):
        k = slot + 3

        @pl.when(k < chunks)
        def _():
            forward(k)
            sent(k - 3)

        @pl.when(slot < PIECES)
        def _():
            cross(slot)

    slots = block // (2 * GROUP)

    def factor(i):
        @pl.loop(0, slots)
        def _(slot):
            pass_on(i * slots + slot)
            eliminate_group(work, 2 * slot)
            eliminate_group(work, 2 * slot + 1)

        rows = slice(i * block, (i + 1) * block)
        inverse[rows, rows] = lower_part(work[...])
        return inverse[rows, rows]

    shift_arrived(0)
    arrived(*parts[0])
    work[...] = with_diagonal(pivots[0], shift[0, 0:1, :])
    first = factor(0)
    inverse[0:block, block:] = jnp.zeros_like(first)
    shift_arrived(1)
    arrived(*parts[1])
    arrived(*parts[2])
    below[...] = dot(pivots[1], first, ((1,), (1,)))
    work[...] = with_diagonal(pivots[2], shift[1, 0:1, :]) - dot(
        below[...], below[...], ((1,), (1,))
    )
    second = factor(1)
    inverse[block:, 0:block] = -dot(
        second, dot(below[...], inverse[0:block, 0:block], ((1,), (0,))), ((1,), (0,))
    )

    @pl.loop(2 * slots, max(chunks - 3, 2 * slots))
    def _(slot):
        pass_on(slot)

    for i, owner, source in parts:
        @pl.when(p == owner)
        def _():
            for d in range(1, n_prow):
                pivot_copy(i, d, source).wait_send()

    for i in (0, 1):
        @pl.when(p == i)
        def _():
            for d in range(1, n_prow):
                shift_copy(i, d).wait_send()

    @pl.loop(0, PIECES)
    def _(piece):
        for s in (0, 1):
            for way, goes in enumerate(ways(s)):
                @pl.when(goes)
                def _():
                    cross_copy(s, piece, way).wait_send()

    @pl.loop(chunks - 3, chunks)
    def _(k):
        sent(k)

    @pl.loop(1, chunks)
    def _(k):
        from_mate(k).wait_recv()


def halves(x):
    high = x.astype(jnp.bfloat16)
    return high, (x - high.astype(jnp.float32)).astype(jnp.bfloat16)


def update_kernel(n_prow, n_pcol, matrix, panel, across, inverse, out, right):
    step = pl.program_id(0)
    blocks, size, col_blocks, _ = matrix.shape

    @pl.when(step == 0)
    def _():
        panels = [
            jnp.concatenate(
                [across[s, pl.ds(c, size, stride=col_blocks), :] for c in range(col_blocks)],
                axis=1,
            )
            for s in (0, 1)
        ]
        solved = dot(inverse[...], jnp.concatenate(panels, axis=0), ((1,), (0,)))
        high, low = halves(solved)
        for j, piece in enumerate((high, low, high)):
            right[2 * j * size:2 * (j + 1) * size, :] = piece

    raw = jnp.concatenate(
        [panel[s].reshape(blocks * size, size) for s in (0, 1)], axis=1
    )
    high, low = halves(dot(raw, inverse[...], ((1,), (1,))))
    left = jnp.concatenate([high, high, low], axis=1)
    product = jnp.dot(left, right[...], preferred_element_type=jnp.float32)
    product = product.reshape(blocks, size, col_blocks, size)
    p = lax.axis_index("prow")
    col = lax.broadcasted_iota(jnp.int32, (1, col_blocks, size), 1) * n_pcol
    cols_kept = col + lax.axis_index("pcol") >= 2
    for b in range(blocks):
        kept = cols_kept & ((step * blocks + b) * n_prow + p >= 2)
        out[b] = jnp.where(kept, matrix[b] - product[b], 0.0)


def on_device(n_prow, n_pcol, coupling, diagonal):
    chunks, size, col_blocks, _ = coupling.shape
    root = math.isqrt(n_prow)
    width = root if root * root == n_prow else n_prow
    f32 = jnp.float32
    dma = pltpu.SemaphoreType.DMA
    vmem = pl.BlockSpec(memory_space=pltpu.VMEM)
    own_shift = jnp.broadcast_to(diagonal[0], (8, size))
    panel, across, inverse = pl.pallas_call(
        functools.partial(share_kernel, n_prow, n_pcol, width),
        out_shape=(
            jax.ShapeDtypeStruct((2, chunks, size, size), f32),
            jax.ShapeDtypeStruct((2, size, col_blocks, size), f32),
            jax.ShapeDtypeStruct((2 * size, 2 * size), f32),
        ),
        in_specs=[pl.BlockSpec(memory_space=pl.ANY), vmem],
        out_specs=(vmem,) * 3,
        scratch_shapes=[
            pltpu.VMEM((3, size, size), f32),
            pltpu.VMEM((2, 8, size), f32),
            pltpu.VMEM((size, size), f32),
            pltpu.VMEM((size, size), f32),
            pltpu.VMEM(coupling.shape, f32),
            dma((chunks,)), dma((4,)), dma((chunks,)), dma((chunks,)), dma((chunks,)), dma((chunks,)),
            dma((3, n_prow)), dma((3,)), dma((3,)),
            dma((2, PIECES, 3)), dma((2, PIECES)), dma((2, n_prow)), dma((2,)),
        ],
        compiler_params=pltpu.CompilerParams(
            collective_id=0, has_side_effects=True, vmem_limit_bytes=60 * 1024 * 1024
        ),
        name="share_panels",
    )(coupling, own_shift)
    blocks = math.gcd(chunks, 4)
    return pl.pallas_call(
        functools.partial(update_kernel, n_prow, n_pcol),
        grid=(chunks // blocks,),
        out_shape=jax.ShapeDtypeStruct(coupling.shape, f32),
        in_specs=[
            pl.BlockSpec((blocks, size, col_blocks, size), lambda i: (i, 0, 0, 0)),
            pl.BlockSpec((2, blocks, size, size), lambda i: (0, i, 0, 0)),
            pl.BlockSpec((2, size * col_blocks, size), lambda i: (0, 0, 0)),
            pl.BlockSpec((2 * size, 2 * size), lambda i: (0, 0)),
        ],
        out_specs=pl.BlockSpec((blocks, size, col_blocks, size), lambda i: (i, 0, 0, 0)),
        scratch_shapes=[pltpu.VMEM((6 * size, col_blocks * size), jnp.bfloat16)],
        compiler_params=pltpu.CompilerParams(vmem_limit_bytes=60 * 1024 * 1024),
        name="update_trailing",
    )(coupling, panel, across.reshape(2, size * col_blocks, size), inverse)


def solution(mesh):
    return jax.shard_map(
        functools.partial(on_device, mesh.shape["prow"], mesh.shape["pcol"]),
        mesh=mesh,
        in_specs=(P(None, "prow", None, "pcol"), P(None, "prow")),
        out_specs=P(None, "prow", None, "pcol"),
        check_vma=False,
    )
```

```python
import functools
import math

import jax
import jax.numpy as jnp
from jax import lax
from jax.experimental import pallas as pl
from jax.experimental.pallas import tpu as pltpu
from jax.sharding import PartitionSpec as P

HIGHEST = lax.Precision.HIGHEST
MESH = pl.DeviceIdType.MESH
GROUP = 8
PIECES = 4
SLOT = 4


def dot(a, b, contract):
    return lax.dot_general(
        a, b, (contract, ((), ())), precision=HIGHEST, preferred_element_type=jnp.float32
    )


def thirds(x):
    first = x.astype(jnp.bfloat16).astype(jnp.float32)
    rest = x - first
    second = rest.astype(jnp.bfloat16).astype(jnp.float32)
    return first, second, rest - second


def halves(x):
    high = x.astype(jnp.bfloat16)
    return high, (x - high.astype(jnp.float32)).astype(jnp.bfloat16)


def eliminate_group(work, group):
    size = work.shape[0]
    start = pl.multiple_of(group * GROUP, GROUP)
    lane = lax.broadcasted_iota(jnp.int32, (GROUP, size), 1) - start
    sub = lax.broadcasted_iota(jnp.int32, (GROUP, size), 0)
    rows = work[pl.ds(start, GROUP), :]
    cols = [
        jnp.broadcast_to(
            jnp.sum(jnp.where(lane == j, rows, 0.0), axis=1, keepdims=True), (GROUP, size)
        )
        for j in range(GROUP)
    ]
    own = (lane >= 0) & (lane < GROUP)
    rows = jnp.where(own, jnp.where(lane == sub, 1.0, 0.0), rows)
    for j in range(GROUP):
        scale = lax.rsqrt(cols[j][j:j + 1, :])
        row = rows[j:j + 1, :] * scale
        column = jnp.where(sub > j, cols[j] * scale, 0.0)
        rows = jnp.where(sub == j, row, rows - column * row)
        for m in range(j + 1, GROUP):
            cols[m] = cols[m] - column * (cols[m][j:j + 1, :] * scale)
    work[pl.ds(start, GROUP), :] = rows
    upper = jnp.where(lane >= GROUP, rows, 0.0)
    a1, a2, a3 = thirds(upper)
    b1, b2, b3 = thirds(rows)
    left = jnp.concatenate([a1, a1, a2, a2, a1, a3], axis=0).astype(jnp.bfloat16)
    right = jnp.concatenate([b1, b2, b1, b2, b3, b1], axis=0).astype(jnp.bfloat16)
    product = lax.dot_general(
        left, right, (((0,), (0,)), ((), ())), preferred_element_type=jnp.float32
    )
    lane_all = lax.broadcasted_iota(jnp.int32, (size, size), 1) - start
    row_all = lax.broadcasted_iota(jnp.int32, (size, size), 0) - start
    dead = (row_all >= GROUP) & (lane_all >= 0) & (lane_all < GROUP)
    work[...] = jnp.where(dead, 0.0, work[...]) - product


def lower_part(x):
    size = x.shape[0]
    row = lax.broadcasted_iota(jnp.int32, (size, size), 0)
    col = lax.broadcasted_iota(jnp.int32, (size, size), 1)
    return jnp.where(row >= col, x, 0.0)


def with_diagonal(block, shift_row):
    size = block.shape[0]
    row = lax.broadcasted_iota(jnp.int32, (size, size), 0)
    col = lax.broadcasted_iota(jnp.int32, (size, size), 1)
    return jnp.where(row == col, block + shift_row, block)


def share_kernel(
    n_prow, n_pcol, width, coupling, own_shift, panel, inverse, right,
    across, pivots, shift, work, below, stage, stage_sem, local_sem, next_send, next_recv, mate_send, mate_recv,
    pivot_send, pivot_recv, pivot_local, cross_send, cross_recv, shift_send, shift_recv,
):
    p = lax.axis_index("prow")
    q = lax.axis_index("pcol")
    chunks, block = coupling.shape[:2]
    height = n_prow // width
    side = q % 2
    mate = q + 1 - 2 * side
    other = 1 - side
    y = p // width
    x = p % width

    barrier = pltpu.get_barrier_semaphore()
    for d in range(1, n_prow):
        pl.semaphore_signal(
            barrier, inc=1, device_id={"prow": (p + d) % n_prow}, device_id_type=MESH
        )
    pl.semaphore_signal(barrier, inc=1, device_id={"pcol": mate}, device_id_type=MESH)

    @pl.when(q >= 2)
    def _():
        pl.semaphore_signal(barrier, inc=1, device_id={"pcol": q - 2}, device_id_type=MESH)

    @pl.when(q + 2 < n_pcol)
    def _():
        pl.semaphore_signal(barrier, inc=1, device_id={"pcol": q + 2}, device_id_type=MESH)

    def staged(k):
        return pltpu.make_async_copy(coupling.at[k], stage.at[k], stage_sem.at[k])

    own_across = pltpu.make_async_copy(coupling.at[0], across.at[p % 2], local_sem.at[1])

    @pl.when(q < 2)
    def _():
        @pl.loop(0, chunks)
        def _(k):
            staged(k).start()

    @pl.when(p < 2)
    def _():
        own_across.start()

    @pl.when(p < 2)
    def _():
        own_across.wait()

    pl.semaphore_wait(
        barrier,
        n_prow + jnp.where(q >= 2, 1, 0) + jnp.where(q + 2 < n_pcol, 1, 0),
    )

    def to_next(k):
        return pltpu.make_async_remote_copy(
            src_ref=panel.at[side, k], dst_ref=panel.at[side, k],
            send_sem=next_send.at[k], recv_sem=next_recv.at[k],
            device_id={"pcol": jnp.minimum(q + 2, n_pcol - 2 + side)}, device_id_type=MESH,
        )

    def to_mate(k):
        return pltpu.make_async_remote_copy(
            src_ref=panel.at[side, k], dst_ref=panel.at[side, k],
            send_sem=mate_send.at[k], recv_sem=mate_recv.at[k],
            device_id={"pcol": mate}, device_id_type=MESH,
        )

    def from_mate(k):
        return pltpu.make_async_remote_copy(
            src_ref=panel.at[other, k], dst_ref=panel.at[other, k],
            send_sem=mate_send.at[k], recv_sem=mate_recv.at[k],
            device_id={"pcol": mate}, device_id_type=MESH,
        )

    def forward(k):
        @pl.when(q < 2)
        def _():
            staged(k).wait()
            panel[side, k] = stage[k, :, 0, :]

        @pl.when(q >= 2)
        def _():
            to_next(k).wait_recv()

        @pl.when(q + 2 < n_pcol)
        def _():
            to_next(k).start()

        to_mate(k).start()

    def sent(k):
        @pl.when(q + 2 < n_pcol)
        def _():
            to_next(k).wait_send()

        to_mate(k).wait_send()

    def pivot_copy(i, d, source):
        return pltpu.make_async_remote_copy(
            src_ref=panel.at[source, 0], dst_ref=pivots.at[i],
            send_sem=pivot_send.at[i, d], recv_sem=pivot_recv.at[i],
            device_id={"prow": (p + d) % n_prow}, device_id_type=MESH,
        )

    parts = ((0, 0, 0), (1, 1, 0), (2, 1, 1))

    def shift_copy(i, d):
        return pltpu.make_async_remote_copy(
            src_ref=own_shift, dst_ref=shift.at[i],
            send_sem=shift_send.at[i, d], recv_sem=shift_recv.at[i],
            device_id={"prow": (p + d) % n_prow}, device_id_type=MESH,
        )

    def shift_local(i):
        return pltpu.make_async_copy(own_shift, shift.at[i], local_sem.at[2 + i])

    def cross_copy(s, piece, way):
        rows = block // PIECES
        part = across.at[s, pl.ds(piece * rows, rows)]
        step = (width, 1, -1)[way]
        return pltpu.make_async_remote_copy(
            src_ref=part, dst_ref=part,
            send_sem=cross_send.at[s, piece, way], recv_sem=cross_recv.at[s, piece],
            device_id={"prow": (p + step + n_prow) % n_prow}, device_id_type=MESH,
        )

    def ways(s):
        return (
            (x == s) & (y + 1 < height),
            (x >= s) & (x + 1 < width),
            (x <= s) & (x >= 1),
        )

    def cross_start(s, piece):
        for way, goes in enumerate(ways(s)):
            @pl.when(goes)
            def _():
                cross_copy(s, piece, way).start()

    def cross(piece):
        for s in (0, 1):
            @pl.when(p != s)
            def _():
                cross_copy(s, piece, 0).wait_recv()
                cross_start(s, piece)

    forward(0)
    for i in (0, 1):
        @pl.when(p == i)
        def _():
            for d in range(1, n_prow):
                shift_copy(i, d).start()
            shift_local(i).start()

    from_mate(0).wait_recv()
    for i, owner, source in parts:
        @pl.when(p == owner)
        def _():
            for d in range(1, n_prow):
                pivot_copy(i, d, source).start()
            pltpu.make_async_copy(panel.at[source, 0], pivots.at[i], pivot_local.at[i]).start()

    early = min(3, chunks)

    @pl.loop(1, early)
    def _(k):
        forward(k)

    @pl.when(q < 2)
    def _():
        @pl.loop(early, chunks)
        def _(k):
            forward(k)

    for s in (0, 1):
        @pl.when(p == s)
        def _():
            @pl.loop(0, PIECES)
            def _(piece):
                cross_start(s, piece)

    def arrived(i, owner, source):
        @pl.when(p == owner)
        def _():
            pltpu.make_async_copy(panel.at[source, 0], pivots.at[i], pivot_local.at[i]).wait()

        @pl.when(p != owner)
        def _():
            pivot_copy(i, 1, source).wait_recv()

    def shift_arrived(i):
        @pl.when(p == i)
        def _():
            shift_local(i).wait()

        @pl.when(p != i)
        def _():
            shift_copy(i, 1).wait_recv()

    slots = block // (SLOT * GROUP)

    def pass_on(slot):
        k = slot + early

        @pl.when((q >= 2) & (k < chunks))
        def _():
            forward(k)

        @pl.when((slot >= 2 * slots - PIECES) & (slot < 2 * slots))
        def _():
            cross(slot - (2 * slots - PIECES))

    def factor(i):
        @pl.loop(0, slots)
        def _(slot):
            pass_on(i * slots + slot)

            @pl.loop(0, SLOT)
            def _(part):
                eliminate_group(work, slot * SLOT + part)

        rows = slice(i * block, (i + 1) * block)
        inverse[rows, rows] = lower_part(work[...])
        return inverse[rows, rows]

    shift_arrived(0)
    arrived(*parts[0])
    work[...] = with_diagonal(pivots[0], shift[0, 0:1, :])
    first = factor(0)
    inverse[0:block, block:] = jnp.zeros_like(first)
    shift_arrived(1)
    arrived(*parts[1])
    arrived(*parts[2])
    below[...] = dot(pivots[1], first, ((1,), (1,)))
    work[...] = with_diagonal(pivots[2], shift[1, 0:1, :]) - dot(
        below[...], below[...], ((1,), (1,))
    )
    second = factor(1)
    inverse[block:, 0:block] = -dot(
        second, dot(below[...], inverse[0:block, 0:block], ((1,), (0,))), ((1,), (0,))
    )

    pass_on(2 * slots)
    panels = [
        jnp.concatenate([across[s, :, c, :] for c in range(across.shape[2])], axis=1)
        for s in (0, 1)
    ]
    solved = dot(inverse[...], jnp.concatenate(panels, axis=0), ((1,), (0,)))
    high, low = halves(solved)
    for j, piece in enumerate((high, low, high)):
        right[2 * j * block:2 * (j + 1) * block, :] = piece

    @pl.loop(2 * slots + 1, max(chunks - early, 2 * slots + 1))
    def _(slot):
        pass_on(slot)

    for i, owner, source in parts:
        @pl.when(p == owner)
        def _():
            for d in range(1, n_prow):
                pivot_copy(i, d, source).wait_send()

    for i in (0, 1):
        @pl.when(p == i)
        def _():
            for d in range(1, n_prow):
                shift_copy(i, d).wait_send()

    @pl.loop(0, PIECES)
    def _(piece):
        for s in (0, 1):
            for way, goes in enumerate(ways(s)):
                @pl.when(goes)
                def _():
                    cross_copy(s, piece, way).wait_send()

    @pl.loop(0, chunks)
    def _(k):
        sent(k)

    @pl.loop(1, chunks)
    def _(k):
        from_mate(k).wait_recv()


def update_kernel(n_prow, n_pcol, matrix, panel, inverse, right, out):
    step = pl.program_id(0)
    blocks, size, col_blocks, _ = matrix.shape

    raw = jnp.concatenate(
        [panel[s].reshape(blocks * size, size) for s in (0, 1)], axis=1
    )
    high, low = halves(dot(raw, inverse[...], ((1,), (1,))))
    left = jnp.concatenate([high, high, low], axis=1)
    product = jnp.dot(left, right[...], preferred_element_type=jnp.float32)
    product = product.reshape(blocks, size, col_blocks, size)
    p = lax.axis_index("prow")
    col = lax.broadcasted_iota(jnp.int32, (1, col_blocks, size), 1) * n_pcol
    cols_kept = col + lax.axis_index("pcol") >= 2
    for b in range(blocks):
        kept = cols_kept & ((step * blocks + b) * n_prow + p >= 2)
        out[b] = jnp.where(kept, matrix[b] - product[b], 0.0)


def on_device(n_prow, n_pcol, coupling, diagonal):
    chunks, size, col_blocks, _ = coupling.shape
    root = math.isqrt(n_prow)
    width = root if root * root == n_prow else n_prow
    f32 = jnp.float32
    dma = pltpu.SemaphoreType.DMA
    vmem = pl.BlockSpec(memory_space=pltpu.VMEM)
    own_shift = jnp.broadcast_to(diagonal[0], (8, size))
    panel, inverse, right = pl.pallas_call(
        functools.partial(share_kernel, n_prow, n_pcol, width),
        out_shape=(
            jax.ShapeDtypeStruct((2, chunks, size, size), f32),
            jax.ShapeDtypeStruct((2 * size, 2 * size), f32),
            jax.ShapeDtypeStruct((6 * size, col_blocks * size), jnp.bfloat16),
        ),
        in_specs=[pl.BlockSpec(memory_space=pl.ANY), vmem],
        out_specs=(vmem,) * 3,
        scratch_shapes=[
            pltpu.VMEM((2, size, col_blocks, size), f32),
            pltpu.VMEM((3, size, size), f32),
            pltpu.VMEM((2, 8, size), f32),
            pltpu.VMEM((size, size), f32),
            pltpu.VMEM((size, size), f32),
            pltpu.VMEM(coupling.shape, f32),
            dma((chunks,)), dma((4,)), dma((chunks,)), dma((chunks,)), dma((chunks,)), dma((chunks,)),
            dma((3, n_prow)), dma((3,)), dma((3,)),
            dma((2, PIECES, 3)), dma((2, PIECES)), dma((2, n_prow)), dma((2,)),
        ],
        compiler_params=pltpu.CompilerParams(
            collective_id=0, has_side_effects=True, vmem_limit_bytes=60 * 1024 * 1024
        ),
        name="share_panels",
    )(coupling, own_shift)
    blocks = math.gcd(chunks, 4)
    return pl.pallas_call(
        functools.partial(update_kernel, n_prow, n_pcol),
        grid=(chunks // blocks,),
        out_shape=jax.ShapeDtypeStruct(coupling.shape, f32),
        in_specs=[
            pl.BlockSpec((blocks, size, col_blocks, size), lambda i: (i, 0, 0, 0)),
            pl.BlockSpec((2, blocks, size, size), lambda i: (0, i, 0, 0)),
            pl.BlockSpec((2 * size, 2 * size), lambda i: (0, 0)),
            pl.BlockSpec((6 * size, col_blocks * size), lambda i: (0, 0)),
        ],
        out_specs=pl.BlockSpec((blocks, size, col_blocks, size), lambda i: (i, 0, 0, 0)),
        compiler_params=pltpu.CompilerParams(vmem_limit_bytes=60 * 1024 * 1024),
        name="update_trailing",
    )(coupling, panel, inverse, right)


def solution(mesh):
    return jax.shard_map(
        functools.partial(on_device, mesh.shape["prow"], mesh.shape["pcol"]),
        mesh=mesh,
        in_specs=(P(None, "prow", None, "pcol"), P(None, "prow")),
        out_specs=P(None, "prow", None, "pcol"),
        check_vma=False,
    )
```

```python
import functools
import math

import jax
import jax.numpy as jnp
from jax import lax
from jax.experimental import pallas as pl
from jax.experimental.pallas import tpu as pltpu
from jax.sharding import PartitionSpec as P

HIGHEST = lax.Precision.HIGHEST
MESH = pl.DeviceIdType.MESH
GROUP = 8
PIECES = 4
SLOT = 2
QUICK = 4


def dot(a, b, contract):
    return lax.dot_general(
        a, b, (contract, ((), ())), precision=HIGHEST, preferred_element_type=jnp.float32
    )


def thirds(x):
    first = x.astype(jnp.bfloat16).astype(jnp.float32)
    rest = x - first
    second = rest.astype(jnp.bfloat16).astype(jnp.float32)
    return first, second, rest - second


def halves(x):
    high = x.astype(jnp.bfloat16)
    return high, (x - high.astype(jnp.float32)).astype(jnp.bfloat16)


def eliminate_group(work, group):
    size = work.shape[0]
    start = pl.multiple_of(group * GROUP, GROUP)
    lane = lax.broadcasted_iota(jnp.int32, (GROUP, size), 1) - start
    sub = lax.broadcasted_iota(jnp.int32, (GROUP, size), 0)
    rows = work[pl.ds(start, GROUP), :]
    cols = [
        jnp.broadcast_to(
            jnp.sum(jnp.where(lane == j, rows, 0.0), axis=1, keepdims=True), (GROUP, size)
        )
        for j in range(GROUP)
    ]
    own = (lane >= 0) & (lane < GROUP)
    rows = jnp.where(own, jnp.where(lane == sub, 1.0, 0.0), rows)
    for j in range(GROUP):
        scale = lax.rsqrt(cols[j][j:j + 1, :])
        row = rows[j:j + 1, :] * scale
        column = jnp.where(sub > j, cols[j] * scale, 0.0)
        rows = jnp.where(sub == j, row, rows - column * row)
        for m in range(j + 1, GROUP):
            cols[m] = cols[m] - column * (cols[m][j:j + 1, :] * scale)
    work[pl.ds(start, GROUP), :] = rows
    upper = jnp.where(lane >= GROUP, rows, 0.0)
    a1, a2, a3 = thirds(upper)
    b1, b2, b3 = thirds(rows)
    left = jnp.concatenate([a1, a1, a2, a2, a1, a3], axis=0).astype(jnp.bfloat16)
    right = jnp.concatenate([b1, b2, b1, b2, b3, b1], axis=0).astype(jnp.bfloat16)
    product = lax.dot_general(
        left, right, (((0,), (0,)), ((), ())), preferred_element_type=jnp.float32
    )
    lane_all = lax.broadcasted_iota(jnp.int32, (size, size), 1) - start
    row_all = lax.broadcasted_iota(jnp.int32, (size, size), 0) - start
    dead = (row_all >= GROUP) & (lane_all >= 0) & (lane_all < GROUP)
    work[...] = jnp.where(dead, 0.0, work[...]) - product


def lower_part(x):
    size = x.shape[0]
    row = lax.broadcasted_iota(jnp.int32, (size, size), 0)
    col = lax.broadcasted_iota(jnp.int32, (size, size), 1)
    return jnp.where(row >= col, x, 0.0)


def with_diagonal(block, shift_row):
    size = block.shape[0]
    row = lax.broadcasted_iota(jnp.int32, (size, size), 0)
    col = lax.broadcasted_iota(jnp.int32, (size, size), 1)
    return jnp.where(row == col, block + shift_row, block)


def share_kernel(
    n_prow, n_pcol, width, coupling, diagonal, left, right,
    panel, inverse, across, pivots, shift, work, below, stage, stage_sem, local_sem, next_send, next_recv, mate_send, mate_recv,
    pivot_send, pivot_recv, pivot_local, cross_send, cross_recv, shift_send, shift_recv,
):
    p = lax.axis_index("prow")
    q = lax.axis_index("pcol")
    chunks, block = coupling.shape[:2]
    height = n_prow // width
    side = q % 2
    mate = q + 1 - 2 * side
    other = 1 - side
    y = p // width
    x = p % width

    barrier = pltpu.get_barrier_semaphore()
    for d in range(1, n_prow):
        pl.semaphore_signal(
            barrier, inc=1, device_id={"prow": (p + d) % n_prow}, device_id_type=MESH
        )
    pl.semaphore_signal(barrier, inc=1, device_id={"pcol": mate}, device_id_type=MESH)

    @pl.when(q >= 2)
    def _():
        pl.semaphore_signal(barrier, inc=1, device_id={"pcol": q - 2}, device_id_type=MESH)

    @pl.when(q + 2 < n_pcol)
    def _():
        pl.semaphore_signal(barrier, inc=1, device_id={"pcol": q + 2}, device_id_type=MESH)

    def staged(k):
        return pltpu.make_async_copy(coupling.at[k], stage.at[k], stage_sem.at[k])

    own_across = pltpu.make_async_copy(coupling.at[0], across.at[p % 2], local_sem.at[1])

    @pl.when(q < 2)
    def _():
        @pl.loop(0, chunks)
        def _(k):
            staged(k).start()

    @pl.when(p < 2)
    def _():
        own_across.start()

    @pl.when(p < 2)
    def _():
        own_across.wait()

    pl.semaphore_wait(
        barrier,
        n_prow + jnp.where(q >= 2, 1, 0) + jnp.where(q + 2 < n_pcol, 1, 0),
    )

    def to_next(k):
        return pltpu.make_async_remote_copy(
            src_ref=panel.at[side, k], dst_ref=panel.at[side, k],
            send_sem=next_send.at[k], recv_sem=next_recv.at[k],
            device_id={"pcol": jnp.minimum(q + 2, n_pcol - 2 + side)}, device_id_type=MESH,
        )

    def to_mate(k):
        return pltpu.make_async_remote_copy(
            src_ref=panel.at[side, k], dst_ref=panel.at[side, k],
            send_sem=mate_send.at[k], recv_sem=mate_recv.at[k],
            device_id={"pcol": mate}, device_id_type=MESH,
        )

    def from_mate(k):
        return pltpu.make_async_remote_copy(
            src_ref=panel.at[other, k], dst_ref=panel.at[other, k],
            send_sem=mate_send.at[k], recv_sem=mate_recv.at[k],
            device_id={"pcol": mate}, device_id_type=MESH,
        )

    def forward(k):
        @pl.when(q < 2)
        def _():
            staged(k).wait()
            panel[side, k] = stage[k, :, 0, :]

        @pl.when(q >= 2)
        def _():
            to_next(k).wait_recv()

        @pl.when(q + 2 < n_pcol)
        def _():
            to_next(k).start()

        to_mate(k).start()

    def sent(k):
        @pl.when(q + 2 < n_pcol)
        def _():
            to_next(k).wait_send()

        to_mate(k).wait_send()

    def pivot_copy(i, d, source):
        return pltpu.make_async_remote_copy(
            src_ref=panel.at[source, 0], dst_ref=pivots.at[i],
            send_sem=pivot_send.at[i, d], recv_sem=pivot_recv.at[i],
            device_id={"prow": (p + d) % n_prow}, device_id_type=MESH,
        )

    parts = ((0, 0, 0), (1, 1, 0), (2, 1, 1))

    def shift_copy(i, d):
        return pltpu.make_async_remote_copy(
            src_ref=diagonal.at[0:8], dst_ref=shift.at[i],
            send_sem=shift_send.at[i, d], recv_sem=shift_recv.at[i],
            device_id={"prow": (p + d) % n_prow}, device_id_type=MESH,
        )

    def shift_local(i):
        return pltpu.make_async_copy(diagonal.at[0:8], shift.at[i], local_sem.at[2 + i])

    def cross_copy(s, piece, way):
        rows = block // PIECES
        part = across.at[s, pl.ds(piece * rows, rows)]
        step = (width, 1, -1)[way]
        return pltpu.make_async_remote_copy(
            src_ref=part, dst_ref=part,
            send_sem=cross_send.at[s, piece, way], recv_sem=cross_recv.at[s, piece],
            device_id={"prow": (p + step + n_prow) % n_prow}, device_id_type=MESH,
        )

    def ways(s):
        return (
            (x == s) & (y + 1 < height),
            (x >= s) & (x + 1 < width),
            (x <= s) & (x >= 1),
        )

    def cross_start(s, piece):
        for way, goes in enumerate(ways(s)):
            @pl.when(goes)
            def _():
                cross_copy(s, piece, way).start()

    def passes_on(s):
        first, second, third = ways(s)
        return first | second | third

    def cross_relay(piece):
        for s in (0, 1):
            @pl.when((p != s) & passes_on(s))
            def _():
                cross_copy(s, piece, 0).wait_recv()
                cross_start(s, piece)

    def cross_end(piece):
        for s in (0, 1):
            @pl.when((p != s) & jnp.logical_not(passes_on(s)))
            def _():
                cross_copy(s, piece, 0).wait_recv()

    forward(0)
    for i in (0, 1):
        @pl.when(p == i)
        def _():
            for d in range(1, n_prow):
                shift_copy(i, d).start()
            shift_local(i).start()

    from_mate(0).wait_recv()
    for i, owner, source in parts:
        @pl.when(p == owner)
        def _():
            for d in range(1, n_prow):
                pivot_copy(i, d, source).start()
            pltpu.make_async_copy(panel.at[source, 0], pivots.at[i], pivot_local.at[i]).start()

    early = min(3, chunks)

    @pl.loop(1, early)
    def _(k):
        forward(k)

    @pl.when(q < 2)
    def _():
        @pl.loop(early, chunks)
        def _(k):
            forward(k)

    for s in (0, 1):
        @pl.when(p == s)
        def _():
            @pl.loop(0, PIECES)
            def _(piece):
                cross_start(s, piece)

    def arrived(i, owner, source):
        @pl.when(p == owner)
        def _():
            pltpu.make_async_copy(panel.at[source, 0], pivots.at[i], pivot_local.at[i]).wait()

        @pl.when(p != owner)
        def _():
            pivot_copy(i, 1, source).wait_recv()

    def shift_arrived(i):
        @pl.when(p == i)
        def _():
            shift_local(i).wait()

        @pl.when(p != i)
        def _():
            shift_copy(i, 1).wait_recv()

    slots = block // (SLOT * GROUP)

    def pass_on(slot):
        k = early + jnp.where(slot < QUICK, slot, (slot + QUICK) // 2)

        @pl.when((q >= 2) & (k < chunks) & ((slot < QUICK) | (slot % 2 == 0)))
        def _():
            forward(k)

        @pl.when((slot % 3 == 0) & (slot >= 3) & (slot < 3 + 3 * PIECES))
        def _():
            cross_relay(slot // 3 - 1)

    def factor(i):
        @pl.loop(0, slots)
        def _(slot):
            pass_on(i * slots + slot)

            @pl.loop(0, SLOT)
            def _(part):
                eliminate_group(work, slot * SLOT + part)

        rows = slice(i * block, (i + 1) * block)
        inverse[rows, rows] = lower_part(work[...])
        return inverse[rows, rows]

    shift_arrived(0)
    arrived(*parts[0])
    work[...] = with_diagonal(pivots[0], shift[0, 0:1, :])
    first = factor(0)
    inverse[0:block, block:] = jnp.zeros_like(first)
    shift_arrived(1)
    arrived(*parts[1])
    arrived(*parts[2])
    below[...] = dot(pivots[1], first, ((1,), (1,)))
    work[...] = with_diagonal(pivots[2], shift[1, 0:1, :]) - dot(
        below[...], below[...], ((1,), (1,))
    )
    second = factor(1)
    inverse[block:, 0:block] = -dot(
        second, dot(below[...], inverse[0:block, 0:block], ((1,), (0,))), ((1,), (0,))
    )

    @pl.loop(0, PIECES)
    def _(piece):
        cross_end(piece)

    panels = [
        jnp.concatenate([across[s, :, c, :] for c in range(across.shape[2])], axis=1)
        for s in (0, 1)
    ]
    solved = dot(inverse[...], jnp.concatenate(panels, axis=0), ((1,), (0,)))
    high, low = halves(solved)
    for j, piece in enumerate((high, low, high)):
        right[2 * j * block:2 * (j + 1) * block, :] = piece

    done = min(early + (2 * slots + QUICK) // 2, chunks)

    @pl.loop(0, chunks // 2)
    def _(pair):
        for k in (2 * pair, 2 * pair + 1):
            @pl.when((q >= 2) & (k + done < chunks))
            def _():
                forward(k + done)

            @pl.when(k > 0)
            def _():
                from_mate(k).wait_recv()

        raw = jnp.concatenate(
            [
                jnp.concatenate([panel[0, k], panel[1, k]], axis=1)
                for k in (2 * pair, 2 * pair + 1)
            ],
            axis=0,
        )
        solved_rows = jnp.concatenate(halves(dot(raw, inverse[...], ((1,), (1,)))), axis=1)
        left[2 * pair] = solved_rows[0:block]
        left[2 * pair + 1] = solved_rows[block:]

    for i, owner, source in parts:
        @pl.when(p == owner)
        def _():
            for d in range(1, n_prow):
                pivot_copy(i, d, source).wait_send()

    for i in (0, 1):
        @pl.when(p == i)
        def _():
            for d in range(1, n_prow):
                shift_copy(i, d).wait_send()

    @pl.loop(0, PIECES)
    def _(piece):
        for s in (0, 1):
            for way, goes in enumerate(ways(s)):
                @pl.when(goes)
                def _():
                    cross_copy(s, piece, way).wait_send()

    @pl.loop(0, chunks)
    def _(k):
        sent(k)


def update_kernel(n_prow, n_pcol, matrix, left, right, out):
    step = pl.program_id(0)
    blocks, size, col_blocks, _ = matrix.shape

    rows = left[...].reshape(blocks * size, 4 * size)
    rows = jnp.concatenate([rows[:, 0:2 * size], rows], axis=1)
    product = jnp.dot(rows, right[...], preferred_element_type=jnp.float32)
    product = product.reshape(blocks, size, col_blocks, size)
    p = lax.axis_index("prow")
    col = lax.broadcasted_iota(jnp.int32, (1, col_blocks, size), 1) * n_pcol
    cols_kept = col + lax.axis_index("pcol") >= 2
    for b in range(blocks):
        kept = cols_kept & ((step * blocks + b) * n_prow + p >= 2)
        out[b] = jnp.where(kept, matrix[b] - product[b], 0.0)


def on_device(n_prow, n_pcol, coupling, diagonal):
    chunks, size, col_blocks, _ = coupling.shape
    root = math.isqrt(n_prow)
    width = root if root * root == n_prow else n_prow
    f32 = jnp.float32
    dma = pltpu.SemaphoreType.DMA
    vmem = pl.BlockSpec(memory_space=pltpu.VMEM)
    left, right = pl.pallas_call(
        functools.partial(share_kernel, n_prow, n_pcol, width),
        out_shape=(
            jax.ShapeDtypeStruct((chunks, size, 4 * size), jnp.bfloat16),
            jax.ShapeDtypeStruct((6 * size, col_blocks * size), jnp.bfloat16),
        ),
        in_specs=[pl.BlockSpec(memory_space=pl.ANY), vmem],
        out_specs=(vmem,) * 2,
        scratch_shapes=[
            pltpu.VMEM((2, chunks, size, size), f32),
            pltpu.VMEM((2 * size, 2 * size), f32),
            pltpu.VMEM((2, size, col_blocks, size), f32),
            pltpu.VMEM((3, size, size), f32),
            pltpu.VMEM((2, 8, size), f32),
            pltpu.VMEM((size, size), f32),
            pltpu.VMEM((size, size), f32),
            pltpu.VMEM(coupling.shape, f32),
            dma((chunks,)), dma((4,)), dma((chunks,)), dma((chunks,)), dma((chunks,)), dma((chunks,)),
            dma((3, n_prow)), dma((3,)), dma((3,)),
            dma((2, PIECES, 3)), dma((2, PIECES)), dma((2, n_prow)), dma((2,)),
        ],
        compiler_params=pltpu.CompilerParams(
            collective_id=0, has_side_effects=True, vmem_limit_bytes=60 * 1024 * 1024
        ),
        name="share_panels",
    )(coupling, diagonal)
    blocks = math.gcd(chunks, 4)
    return pl.pallas_call(
        functools.partial(update_kernel, n_prow, n_pcol),
        grid=(chunks // blocks,),
        out_shape=jax.ShapeDtypeStruct(coupling.shape, f32),
        in_specs=[
            pl.BlockSpec((blocks, size, col_blocks, size), lambda i: (i, 0, 0, 0)),
            pl.BlockSpec((blocks, size, 4 * size), lambda i: (i, 0, 0)),
            pl.BlockSpec((6 * size, col_blocks * size), lambda i: (0, 0)),
        ],
        out_specs=pl.BlockSpec((blocks, size, col_blocks, size), lambda i: (i, 0, 0, 0)),
        compiler_params=pltpu.CompilerParams(vmem_limit_bytes=60 * 1024 * 1024),
        name="update_trailing",
    )(coupling, left, right)


def solution(mesh):
    return jax.shard_map(
        functools.partial(on_device, mesh.shape["prow"], mesh.shape["pcol"]),
        mesh=mesh,
        in_specs=(P(None, "prow", None, "pcol"), P(None, "prow")),
        out_specs=P(None, "prow", None, "pcol"),
        check_vma=False,
    )
```

```python
import functools
import math

import jax
import jax.numpy as jnp
from jax import lax
from jax.experimental import pallas as pl
from jax.experimental.pallas import tpu as pltpu
from jax.sharding import PartitionSpec as P

HIGHEST = lax.Precision.HIGHEST
MESH = pl.DeviceIdType.MESH
GROUP = 8
PIECES = 4
SLOT = 2
QUICK = 6
AHEAD = 4


def dot(a, b, contract):
    return lax.dot_general(
        a, b, (contract, ((), ())), precision=HIGHEST, preferred_element_type=jnp.float32
    )


def thirds(x):
    first = x.astype(jnp.bfloat16).astype(jnp.float32)
    rest = x - first
    second = rest.astype(jnp.bfloat16).astype(jnp.float32)
    return first, second, rest - second


def halves(x):
    high = x.astype(jnp.bfloat16)
    return high, (x - high.astype(jnp.float32)).astype(jnp.bfloat16)


def eliminate_group(work, group):
    size = work.shape[0]
    start = pl.multiple_of(group * GROUP, GROUP)
    lane = lax.broadcasted_iota(jnp.int32, (GROUP, size), 1) - start
    sub = lax.broadcasted_iota(jnp.int32, (GROUP, size), 0)
    rows = work[pl.ds(start, GROUP), :]
    cols = [
        jnp.broadcast_to(
            jnp.sum(jnp.where(lane == j, rows, 0.0), axis=1, keepdims=True), (GROUP, size)
        )
        for j in range(GROUP)
    ]
    own = (lane >= 0) & (lane < GROUP)
    rows = jnp.where(own, jnp.where(lane == sub, 1.0, 0.0), rows)
    for j in range(GROUP):
        scale = lax.rsqrt(cols[j][j:j + 1, :])
        row = rows[j:j + 1, :] * scale
        column = jnp.where(sub > j, cols[j] * scale, 0.0)
        rows = jnp.where(sub == j, row, rows - column * row)
        for m in range(j + 1, GROUP):
            cols[m] = cols[m] - column * (cols[m][j:j + 1, :] * scale)
    work[pl.ds(start, GROUP), :] = rows
    upper = jnp.where(lane >= GROUP, rows, 0.0)
    a1, a2, a3 = thirds(upper)
    b1, b2, b3 = thirds(rows)
    left = jnp.concatenate([a1, a1, a2, a2, a1, a3], axis=0).astype(jnp.bfloat16)
    right = jnp.concatenate([b1, b2, b1, b2, b3, b1], axis=0).astype(jnp.bfloat16)
    product = lax.dot_general(
        left, right, (((0,), (0,)), ((), ())), preferred_element_type=jnp.float32
    )
    lane_all = lax.broadcasted_iota(jnp.int32, (size, size), 1) - start
    row_all = lax.broadcasted_iota(jnp.int32, (size, size), 0) - start
    dead = (row_all >= GROUP) & (lane_all >= 0) & (lane_all < GROUP)
    work[...] = jnp.where(dead, 0.0, work[...]) - product


def lower_part(x):
    size = x.shape[0]
    row = lax.broadcasted_iota(jnp.int32, (size, size), 0)
    col = lax.broadcasted_iota(jnp.int32, (size, size), 1)
    return jnp.where(row >= col, x, 0.0)


def with_diagonal(block, shift_row):
    size = block.shape[0]
    row = lax.broadcasted_iota(jnp.int32, (size, size), 0)
    col = lax.broadcasted_iota(jnp.int32, (size, size), 1)
    return jnp.where(row == col, block + shift_row, block)


def share_kernel(
    n_prow, n_pcol, width, coupling, diagonal, left, right,
    left_own, right_own, panel, inverse, across, pivots, shift, work, below, stage,
    left_sem, stage_sem, local_sem, next_send, next_recv, mate_send, mate_recv,
    pivot_send, pivot_recv, pivot_local, cross_send, cross_recv, shift_send, shift_recv,
):
    p = lax.axis_index("prow")
    q = lax.axis_index("pcol")
    chunks, block = coupling.shape[:2]
    height = n_prow // width
    side = q % 2
    mate = q + 1 - 2 * side
    other = 1 - side
    y = p // width
    x = p % width

    barrier = pltpu.get_barrier_semaphore()
    for d in range(1, n_prow):
        pl.semaphore_signal(
            barrier, inc=1, device_id={"prow": (p + d) % n_prow}, device_id_type=MESH
        )
    pl.semaphore_signal(barrier, inc=1, device_id={"pcol": mate}, device_id_type=MESH)

    @pl.when(q >= 2)
    def _():
        pl.semaphore_signal(barrier, inc=1, device_id={"pcol": q - 2}, device_id_type=MESH)

    @pl.when(q + 2 < n_pcol)
    def _():
        pl.semaphore_signal(barrier, inc=1, device_id={"pcol": q + 2}, device_id_type=MESH)

    def staged(k):
        return pltpu.make_async_copy(coupling.at[k], stage.at[k], stage_sem.at[k])

    own_across = pltpu.make_async_copy(coupling.at[0], across.at[p % 2], local_sem.at[1])

    @pl.when(q < 2)
    def _():
        @pl.loop(0, chunks)
        def _(k):
            staged(k).start()

    @pl.when(p < 2)
    def _():
        own_across.start()

    @pl.when(p < 2)
    def _():
        own_across.wait()

    pl.semaphore_wait(
        barrier,
        n_prow + jnp.where(q >= 2, 1, 0) + jnp.where(q + 2 < n_pcol, 1, 0),
    )

    def to_next(k):
        return pltpu.make_async_remote_copy(
            src_ref=panel.at[side, k], dst_ref=panel.at[side, k],
            send_sem=next_send.at[k], recv_sem=next_recv.at[k],
            device_id={"pcol": jnp.minimum(q + 2, n_pcol - 2 + side)}, device_id_type=MESH,
        )

    def to_mate(k):
        return pltpu.make_async_remote_copy(
            src_ref=panel.at[side, k], dst_ref=panel.at[side, k],
            send_sem=mate_send.at[k], recv_sem=mate_recv.at[k],
            device_id={"pcol": mate}, device_id_type=MESH,
        )

    def from_mate(k):
        return pltpu.make_async_remote_copy(
            src_ref=panel.at[other, k], dst_ref=panel.at[other, k],
            send_sem=mate_send.at[k], recv_sem=mate_recv.at[k],
            device_id={"pcol": mate}, device_id_type=MESH,
        )

    def forward(k):
        @pl.when(q < 2)
        def _():
            staged(k).wait()
            panel[side, k] = stage[k, :, 0, :]

        @pl.when(q >= 2)
        def _():
            to_next(k).wait_recv()

        @pl.when(q + 2 < n_pcol)
        def _():
            to_next(k).start()

        to_mate(k).start()

    def sent(k):
        @pl.when(q + 2 < n_pcol)
        def _():
            to_next(k).wait_send()

        to_mate(k).wait_send()

    def pivot_copy(i, d, source):
        return pltpu.make_async_remote_copy(
            src_ref=panel.at[source, 0], dst_ref=pivots.at[i],
            send_sem=pivot_send.at[i, d], recv_sem=pivot_recv.at[i],
            device_id={"prow": (p + d) % n_prow}, device_id_type=MESH,
        )

    parts = ((0, 0, 0), (1, 1, 0), (2, 1, 1))

    def shift_copy(i, d):
        return pltpu.make_async_remote_copy(
            src_ref=diagonal.at[0:8], dst_ref=shift.at[i],
            send_sem=shift_send.at[i, d], recv_sem=shift_recv.at[i],
            device_id={"prow": (p + d) % n_prow}, device_id_type=MESH,
        )

    def shift_local(i):
        return pltpu.make_async_copy(diagonal.at[0:8], shift.at[i], local_sem.at[2 + i])

    def cross_copy(s, piece, way):
        rows = block // PIECES
        part = across.at[s, pl.ds(piece * rows, rows)]
        step = (width, 1, -1)[way]
        return pltpu.make_async_remote_copy(
            src_ref=part, dst_ref=part,
            send_sem=cross_send.at[s, piece, way], recv_sem=cross_recv.at[s, piece],
            device_id={"prow": (p + step + n_prow) % n_prow}, device_id_type=MESH,
        )

    def ways(s):
        return (
            (x == s) & (y + 1 < height),
            (x >= s) & (x + 1 < width),
            (x <= s) & (x >= 1),
        )

    def cross_start(s, piece):
        for way, goes in enumerate(ways(s)):
            @pl.when(goes)
            def _():
                cross_copy(s, piece, way).start()

    def passes_on(s):
        first, second, third = ways(s)
        return first | second | third

    def cross_relay(piece):
        for s in (0, 1):
            @pl.when((p != s) & passes_on(s))
            def _():
                cross_copy(s, piece, 0).wait_recv()
                cross_start(s, piece)

    def cross_end(piece):
        for s in (0, 1):
            @pl.when((p != s) & jnp.logical_not(passes_on(s)))
            def _():
                cross_copy(s, piece, 0).wait_recv()

    forward(0)
    for i in (0, 1):
        @pl.when(p == i)
        def _():
            for d in range(1, n_prow):
                shift_copy(i, d).start()
            shift_local(i).start()

    from_mate(0).wait_recv()
    for i, owner, source in parts:
        @pl.when(p == owner)
        def _():
            for d in range(1, n_prow):
                pivot_copy(i, d, source).start()
            pltpu.make_async_copy(panel.at[source, 0], pivots.at[i], pivot_local.at[i]).start()

    early = 1
    middle = (q >= 2) & (q + 2 < n_pcol)
    last = (q >= 2) & (q + 2 >= n_pcol)

    @pl.when(q < 2)
    def _():
        @pl.loop(early, chunks)
        def _(k):
            forward(k)

    for s in (0, 1):
        @pl.when(p == s)
        def _():
            @pl.loop(0, PIECES)
            def _(piece):
                cross_start(s, piece)

    def arrived(i, owner, source):
        @pl.when(p == owner)
        def _():
            pltpu.make_async_copy(panel.at[source, 0], pivots.at[i], pivot_local.at[i]).wait()

        @pl.when(p != owner)
        def _():
            pivot_copy(i, 1, source).wait_recv()

    def shift_arrived(i):
        @pl.when(p == i)
        def _():
            shift_local(i).wait()

        @pl.when(p != i)
        def _():
            shift_copy(i, 1).wait_recv()

    slots = block // (SLOT * GROUP)

    def pass_on(slot):
        k = early + jnp.where(slot < QUICK, slot, (slot + QUICK) // 2)

        @pl.when(middle & (k < chunks) & ((slot < QUICK) | (slot % 2 == 0)))
        def _():
            forward(k)

        @pl.when((slot % 3 == 0) & (slot >= 3) & (slot < 3 + 3 * PIECES))
        def _():
            cross_relay(slot // 3 - 1)

    def factor(i):
        @pl.loop(0, slots)
        def _(slot):
            pass_on(i * slots + slot)

            @pl.loop(0, SLOT)
            def _(part):
                eliminate_group(work, slot * SLOT + part)

        rows = slice(i * block, (i + 1) * block)
        inverse[rows, rows] = lower_part(work[...])
        return inverse[rows, rows]

    shift_arrived(0)
    arrived(*parts[0])
    work[...] = with_diagonal(pivots[0], shift[0, 0:1, :])
    first = factor(0)
    inverse[0:block, block:] = jnp.zeros_like(first)
    shift_arrived(1)
    arrived(*parts[1])
    arrived(*parts[2])
    below[...] = dot(pivots[1], first, ((1,), (1,)))
    work[...] = with_diagonal(pivots[2], shift[1, 0:1, :]) - dot(
        below[...], below[...], ((1,), (1,))
    )
    second = factor(1)
    done = min(early + (2 * slots + QUICK) // 2, chunks)

    def forward_middle(start, stop):
        for k in range(min(start, chunks), min(stop, chunks)):
            @pl.when(middle)
            def _():
                forward(k)

    forward_middle(done, done + 2)
    inverse[block:, 0:block] = -dot(
        second, dot(below[...], inverse[0:block, 0:block], ((1,), (0,))), ((1,), (0,))
    )
    forward_middle(done + 2, done + 3)

    @pl.loop(0, PIECES)
    def _(piece):
        cross_end(piece)

    panels = [
        jnp.concatenate([across[s, :, c, :] for c in range(across.shape[2])], axis=1)
        for s in (0, 1)
    ]
    solved = dot(inverse[...], jnp.concatenate(panels, axis=0), ((1,), (0,)))
    high, low = halves(solved)
    for j, piece in enumerate((high, low, high)):
        right_own[2 * j * block:2 * (j + 1) * block, :] = piece
    right_copy = pltpu.make_async_copy(right_own, right, local_sem.at[0])
    right_copy.start()
    forward_middle(done + 3, chunks)

    @pl.when(last)
    def _():
        @pl.loop(early, done)
        def _(k):
            forward(k)

    def left_copy(pair):
        part = pl.ds(2 * pair, 2)
        return pltpu.make_async_copy(left_own.at[part], left.at[part], left_sem.at[pair])

    @pl.loop(0, chunks // 2)
    def _(pair):
        for k in (2 * pair, 2 * pair + 1):
            @pl.when(last & (k + AHEAD >= done) & (k + AHEAD < chunks))
            def _():
                forward(k + AHEAD)

            @pl.when(k > 0)
            def _():
                from_mate(k).wait_recv()

        raw = jnp.concatenate(
            [
                jnp.concatenate([panel[0, k], panel[1, k]], axis=1)
                for k in (2 * pair, 2 * pair + 1)
            ],
            axis=0,
        )
        solved_rows = jnp.concatenate(halves(dot(raw, inverse[...], ((1,), (1,)))), axis=1)
        left_own[2 * pair] = solved_rows[0:block]
        left_own[2 * pair + 1] = solved_rows[block:]
        left_copy(pair).start()

    for i, owner, source in parts:
        @pl.when(p == owner)
        def _():
            for d in range(1, n_prow):
                pivot_copy(i, d, source).wait_send()

    for i in (0, 1):
        @pl.when(p == i)
        def _():
            for d in range(1, n_prow):
                shift_copy(i, d).wait_send()

    @pl.loop(0, PIECES)
    def _(piece):
        for s in (0, 1):
            for way, goes in enumerate(ways(s)):
                @pl.when(goes)
                def _():
                    cross_copy(s, piece, way).wait_send()

    @pl.loop(0, chunks)
    def _(k):
        sent(k)

    right_copy.wait()

    @pl.loop(0, chunks // 2)
    def _(pair):
        left_copy(pair).wait()


def update_kernel(n_prow, n_pcol, matrix, left, right, out):
    step = pl.program_id(0)
    blocks, size, col_blocks, _ = matrix.shape

    rows = left[...].reshape(blocks * size, 4 * size)
    rows = jnp.concatenate([rows[:, 0:2 * size], rows], axis=1)
    product = jnp.dot(rows, right[...], preferred_element_type=jnp.float32)
    product = product.reshape(blocks, size, col_blocks, size)
    p = lax.axis_index("prow")
    col = lax.broadcasted_iota(jnp.int32, (1, col_blocks, size), 1) * n_pcol
    cols_kept = col + lax.axis_index("pcol") >= 2
    for b in range(blocks):
        kept = cols_kept & ((step * blocks + b) * n_prow + p >= 2)
        out[b] = jnp.where(kept, matrix[b] - product[b], 0.0)


def on_device(n_prow, n_pcol, coupling, diagonal):
    chunks, size, col_blocks, _ = coupling.shape
    root = math.isqrt(n_prow)
    width = root if root * root == n_prow else n_prow
    f32 = jnp.float32
    dma = pltpu.SemaphoreType.DMA
    vmem = pl.BlockSpec(memory_space=pltpu.VMEM)
    left, right = pl.pallas_call(
        functools.partial(share_kernel, n_prow, n_pcol, width),
        out_shape=(
            jax.ShapeDtypeStruct((chunks, size, 4 * size), jnp.bfloat16),
            jax.ShapeDtypeStruct((6 * size, col_blocks * size), jnp.bfloat16),
        ),
        in_specs=[pl.BlockSpec(memory_space=pl.ANY), vmem],
        out_specs=(pl.BlockSpec(memory_space=pl.ANY),) * 2,
        scratch_shapes=[
            pltpu.VMEM((chunks, size, 4 * size), jnp.bfloat16),
            pltpu.VMEM((6 * size, col_blocks * size), jnp.bfloat16),
            pltpu.VMEM((2, chunks, size, size), f32),
            pltpu.VMEM((2 * size, 2 * size), f32),
            pltpu.VMEM((2, size, col_blocks, size), f32),
            pltpu.VMEM((3, size, size), f32),
            pltpu.VMEM((2, 8, size), f32),
            pltpu.VMEM((size, size), f32),
            pltpu.VMEM((size, size), f32),
            pltpu.VMEM(coupling.shape, f32),
            dma((chunks // 2,)), dma((chunks,)), dma((4,)), dma((chunks,)), dma((chunks,)), dma((chunks,)), dma((chunks,)),
            dma((3, n_prow)), dma((3,)), dma((3,)),
            dma((2, PIECES, 3)), dma((2, PIECES)), dma((2, n_prow)), dma((2,)),
        ],
        compiler_params=pltpu.CompilerParams(
            collective_id=0, has_side_effects=True, vmem_limit_bytes=60 * 1024 * 1024
        ),
        name="share_panels",
    )(coupling, diagonal)
    blocks = math.gcd(chunks, 2)
    return pl.pallas_call(
        functools.partial(update_kernel, n_prow, n_pcol),
        grid=(chunks // blocks,),
        out_shape=jax.ShapeDtypeStruct(coupling.shape, f32),
        in_specs=[
            pl.BlockSpec((blocks, size, col_blocks, size), lambda i: (i, 0, 0, 0)),
            pl.BlockSpec((blocks, size, 4 * size), lambda i: (i, 0, 0)),
            pl.BlockSpec((6 * size, col_blocks * size), lambda i: (0, 0)),
        ],
        out_specs=pl.BlockSpec((blocks, size, col_blocks, size), lambda i: (i, 0, 0, 0)),
        compiler_params=pltpu.CompilerParams(vmem_limit_bytes=60 * 1024 * 1024),
        name="update_trailing",
    )(coupling, left, right)


def solution(mesh):
    return jax.shard_map(
        functools.partial(on_device, mesh.shape["prow"], mesh.shape["pcol"]),
        mesh=mesh,
        in_specs=(P(None, "prow", None, "pcol"), P(None, "prow")),
        out_specs=P(None, "prow", None, "pcol"),
        check_vma=False,
    )
```

```python
import functools
import math

import jax
import jax.numpy as jnp
from jax import lax
from jax.experimental import pallas as pl
from jax.experimental.pallas import tpu as pltpu
from jax.sharding import PartitionSpec as P

HIGHEST = lax.Precision.HIGHEST
MESH = pl.DeviceIdType.MESH
GROUP = 8
PIECES = 4
SLOT = 2
QUICK = 6
CROSS = 2


def dot(a, b, contract):
    return lax.dot_general(
        a, b, (contract, ((), ())), precision=HIGHEST, preferred_element_type=jnp.float32
    )


def thirds(x):
    first = x.astype(jnp.bfloat16).astype(jnp.float32)
    rest = x - first
    second = rest.astype(jnp.bfloat16).astype(jnp.float32)
    return first, second, rest - second


def halves(x):
    high = x.astype(jnp.bfloat16)
    return high, (x - high.astype(jnp.float32)).astype(jnp.bfloat16)


def eliminate_group(work, group):
    size = work.shape[0]
    start = pl.multiple_of(group * GROUP, GROUP)
    lane = lax.broadcasted_iota(jnp.int32, (GROUP, size), 1) - start
    sub = lax.broadcasted_iota(jnp.int32, (GROUP, size), 0)
    rows = work[pl.ds(start, GROUP), :]
    cols = [
        jnp.broadcast_to(
            jnp.sum(jnp.where(lane == j, rows, 0.0), axis=1, keepdims=True), (GROUP, size)
        )
        for j in range(GROUP)
    ]
    own = (lane >= 0) & (lane < GROUP)
    rows = jnp.where(own, jnp.where(lane == sub, 1.0, 0.0), rows)
    for j in range(GROUP):
        scale = lax.rsqrt(cols[j][j:j + 1, :])
        row = rows[j:j + 1, :] * scale
        column = jnp.where(sub > j, cols[j] * scale, 0.0)
        rows = jnp.where(sub == j, row, rows - column * row)
        for m in range(j + 1, GROUP):
            cols[m] = cols[m] - column * (cols[m][j:j + 1, :] * scale)
    work[pl.ds(start, GROUP), :] = rows
    upper = jnp.where(lane >= GROUP, rows, 0.0)
    a1, a2, a3 = thirds(upper)
    b1, b2, b3 = thirds(rows)
    left = jnp.concatenate([a1, a1, a2, a2, a1, a3], axis=0).astype(jnp.bfloat16)
    right = jnp.concatenate([b1, b2, b1, b2, b3, b1], axis=0).astype(jnp.bfloat16)
    product = lax.dot_general(
        left, right, (((0,), (0,)), ((), ())), preferred_element_type=jnp.float32
    )
    lane_all = lax.broadcasted_iota(jnp.int32, (size, size), 1) - start
    row_all = lax.broadcasted_iota(jnp.int32, (size, size), 0) - start
    dead = (row_all >= GROUP) & (lane_all >= 0) & (lane_all < GROUP)
    work[...] = jnp.where(dead, 0.0, work[...]) - product


def lower_part(x):
    size = x.shape[0]
    row = lax.broadcasted_iota(jnp.int32, (size, size), 0)
    col = lax.broadcasted_iota(jnp.int32, (size, size), 1)
    return jnp.where(row >= col, x, 0.0)


def with_diagonal(block, shift_row):
    size = block.shape[0]
    row = lax.broadcasted_iota(jnp.int32, (size, size), 0)
    col = lax.broadcasted_iota(jnp.int32, (size, size), 1)
    return jnp.where(row == col, block + shift_row, block)


def share_kernel(
    n_prow, n_pcol, width, coupling, diagonal, left, right,
    left_own, right_own, panel, inverse, across, pivots, shift, work, below, stage,
    left_sem, stage_sem, local_sem, next_send, next_recv, mate_send, mate_recv,
    pivot_send, pivot_recv, pivot_local, cross_send, cross_recv, shift_send, shift_recv,
):
    p = lax.axis_index("prow")
    q = lax.axis_index("pcol")
    chunks, block = coupling.shape[:2]
    height = n_prow // width
    side = q % 2
    mate = q + 1 - 2 * side
    other = 1 - side
    y = p // width
    x = p % width

    barrier = pltpu.get_barrier_semaphore()
    for d in range(1, n_prow):
        pl.semaphore_signal(
            barrier, inc=1, device_id={"prow": (p + d) % n_prow}, device_id_type=MESH
        )
    pl.semaphore_signal(barrier, inc=1, device_id={"pcol": mate}, device_id_type=MESH)

    @pl.when(q >= 2)
    def _():
        pl.semaphore_signal(barrier, inc=1, device_id={"pcol": q - 2}, device_id_type=MESH)

    @pl.when(q + 2 < n_pcol)
    def _():
        pl.semaphore_signal(barrier, inc=1, device_id={"pcol": q + 2}, device_id_type=MESH)

    def staged(k):
        return pltpu.make_async_copy(coupling.at[k], stage.at[k], stage_sem.at[k])

    own_across = pltpu.make_async_copy(coupling.at[0], across.at[p % 2], local_sem.at[1])

    @pl.when(q < 2)
    def _():
        @pl.loop(0, chunks)
        def _(k):
            staged(k).start()

    @pl.when(p < 2)
    def _():
        own_across.start()

    @pl.when(p < 2)
    def _():
        own_across.wait()

    pl.semaphore_wait(
        barrier,
        n_prow + jnp.where(q >= 2, 1, 0) + jnp.where(q + 2 < n_pcol, 1, 0),
    )

    def to_next(k):
        return pltpu.make_async_remote_copy(
            src_ref=panel.at[side, k], dst_ref=panel.at[side, k],
            send_sem=next_send.at[k], recv_sem=next_recv.at[k],
            device_id={"pcol": jnp.minimum(q + 2, n_pcol - 2 + side)}, device_id_type=MESH,
        )

    def to_mate(k):
        return pltpu.make_async_remote_copy(
            src_ref=panel.at[side, k], dst_ref=panel.at[side, k],
            send_sem=mate_send.at[k], recv_sem=mate_recv.at[k],
            device_id={"pcol": mate}, device_id_type=MESH,
        )

    def from_mate(k):
        return pltpu.make_async_remote_copy(
            src_ref=panel.at[other, k], dst_ref=panel.at[other, k],
            send_sem=mate_send.at[k], recv_sem=mate_recv.at[k],
            device_id={"pcol": mate}, device_id_type=MESH,
        )

    def forward(k):
        @pl.when(q < 2)
        def _():
            staged(k).wait()
            panel[side, k] = stage[k, :, 0, :]

        @pl.when(q >= 2)
        def _():
            to_next(k).wait_recv()

        @pl.when(q + 2 < n_pcol)
        def _():
            to_next(k).start()

        to_mate(k).start()

    def sent(k):
        @pl.when(q + 2 < n_pcol)
        def _():
            to_next(k).wait_send()

        to_mate(k).wait_send()

    def pivot_copy(i, d, source):
        return pltpu.make_async_remote_copy(
            src_ref=panel.at[source, 0], dst_ref=pivots.at[i],
            send_sem=pivot_send.at[i, d], recv_sem=pivot_recv.at[i],
            device_id={"prow": (p + d) % n_prow}, device_id_type=MESH,
        )

    parts = ((0, 0, 0), (1, 1, 0), (2, 1, 1))

    def shift_copy(i, d):
        return pltpu.make_async_remote_copy(
            src_ref=diagonal.at[0:8], dst_ref=shift.at[i],
            send_sem=shift_send.at[i, d], recv_sem=shift_recv.at[i],
            device_id={"prow": (p + d) % n_prow}, device_id_type=MESH,
        )

    def shift_local(i):
        return pltpu.make_async_copy(diagonal.at[0:8], shift.at[i], local_sem.at[2 + i])

    def cross_copy(s, piece, way):
        rows = block // PIECES
        part = across.at[s, pl.ds(piece * rows, rows)]
        step = (width, 1, -1)[way]
        return pltpu.make_async_remote_copy(
            src_ref=part, dst_ref=part,
            send_sem=cross_send.at[s, piece, way], recv_sem=cross_recv.at[s, piece],
            device_id={"prow": (p + step + n_prow) % n_prow}, device_id_type=MESH,
        )

    def ways(s):
        return (
            (x == s) & (y + 1 < height),
            (x >= s) & (x + 1 < width),
            (x <= s) & (x >= 1),
        )

    def cross_start(s, piece):
        for way, goes in enumerate(ways(s)):
            @pl.when(goes)
            def _():
                cross_copy(s, piece, way).start()

    def passes_on(s):
        first, second, third = ways(s)
        return first | second | third

    def cross_relay(piece):
        for s in (0, 1):
            @pl.when((p != s) & passes_on(s))
            def _():
                cross_copy(s, piece, 0).wait_recv()
                cross_start(s, piece)

    def cross_end(piece):
        for s in (0, 1):
            @pl.when((p != s) & jnp.logical_not(passes_on(s)))
            def _():
                cross_copy(s, piece, 0).wait_recv()

    forward(0)
    for i in (0, 1):
        @pl.when(p == i)
        def _():
            for d in range(1, n_prow):
                shift_copy(i, d).start()
            shift_local(i).start()

    from_mate(0).wait_recv()
    for i, owner, source in parts:
        @pl.when(p == owner)
        def _():
            for d in range(1, n_prow):
                pivot_copy(i, d, source).start()
            pltpu.make_async_copy(panel.at[source, 0], pivots.at[i], pivot_local.at[i]).start()

    early = 1
    middle = (q >= 2) & (q + 2 < n_pcol)
    last = (q >= 2) & (q + 2 >= n_pcol)

    @pl.when(q < 2)
    def _():
        @pl.loop(early, chunks)
        def _(k):
            forward(k)

    def arrived(i, owner, source):
        @pl.when(p == owner)
        def _():
            pltpu.make_async_copy(panel.at[source, 0], pivots.at[i], pivot_local.at[i]).wait()

        @pl.when(p != owner)
        def _():
            pivot_copy(i, 1, source).wait_recv()

    def shift_arrived(i):
        @pl.when(p == i)
        def _():
            shift_local(i).wait()

        @pl.when(p != i)
        def _():
            shift_copy(i, 1).wait_recv()

    slots = block // (SLOT * GROUP)

    def pass_on(slot):
        k = early + jnp.where(slot < QUICK, slot, (slot + QUICK) // 2)

        @pl.when(middle & (k < chunks) & ((slot < QUICK) | (slot % 2 == 0)))
        def _():
            forward(k)

        for s in (0, 1):
            @pl.when((p == s) & (slot == CROSS))
            def _():
                @pl.loop(0, PIECES)
                def _(piece):
                    cross_start(s, piece)

        @pl.when((slot % 4 == 3) & (slot >= CROSS + 4))
        def _():
            cross_relay((slot - CROSS) // 4 - 1)

    def factor(i):
        @pl.loop(0, slots)
        def _(slot):
            pass_on(i * slots + slot)

            @pl.loop(0, SLOT)
            def _(part):
                eliminate_group(work, slot * SLOT + part)

        rows = slice(i * block, (i + 1) * block)
        inverse[rows, rows] = lower_part(work[...])
        return inverse[rows, rows]

    shift_arrived(0)
    arrived(*parts[0])
    work[...] = with_diagonal(pivots[0], shift[0, 0:1, :])
    first = factor(0)
    inverse[0:block, block:] = jnp.zeros_like(first)
    shift_arrived(1)
    arrived(*parts[1])
    arrived(*parts[2])
    below[...] = dot(pivots[1], first, ((1,), (1,)))
    work[...] = with_diagonal(pivots[2], shift[1, 0:1, :]) - dot(
        below[...], below[...], ((1,), (1,))
    )
    second = factor(1)
    done = min(early + (2 * slots + QUICK) // 2, chunks)

    def forward_middle(start, stop):
        for k in range(min(start, chunks), min(stop, chunks)):
            @pl.when(middle)
            def _():
                forward(k)

    relayed = (2 * slots - CROSS - 1) // 4
    forward_middle(done, done + 1)
    inverse[block:, 0:block] = -dot(
        second, dot(below[...], inverse[0:block, 0:block], ((1,), (0,))), ((1,), (0,))
    )

    @pl.loop(relayed, PIECES)
    def _(piece):
        cross_relay(piece)

    @pl.when(last)
    def _():
        @pl.loop(early, done)
        def _(k):
            forward(k)

    def left_copy(pair):
        part = pl.ds(2 * pair, 2)
        return pltpu.make_async_copy(left_own.at[part], left.at[part], left_sem.at[pair])

    def solve_rows(pair):
        @pl.when(middle & (pair + done + 1 < chunks))
        def _():
            forward(pair + done + 1)

        for k in (2 * pair, 2 * pair + 1):
            @pl.when(last & (k >= done))
            def _():
                forward(k)

            @pl.when(k > 0)
            def _():
                from_mate(k).wait_recv()

        raw = jnp.concatenate(
            [
                jnp.concatenate([panel[0, k], panel[1, k]], axis=1)
                for k in (2 * pair, 2 * pair + 1)
            ],
            axis=0,
        )
        solved_rows = jnp.concatenate(halves(dot(raw, inverse[...], ((1,), (1,)))), axis=1)
        left_own[2 * pair] = solved_rows[0:block]
        left_own[2 * pair + 1] = solved_rows[block:]
        left_copy(pair).start()

    @pl.loop(0, done // 2)
    def _(pair):
        solve_rows(pair)

    @pl.loop(0, PIECES)
    def _(piece):
        cross_end(piece)

    panels = [
        jnp.concatenate([across[s, :, c, :] for c in range(across.shape[2])], axis=1)
        for s in (0, 1)
    ]
    solved = dot(inverse[...], jnp.concatenate(panels, axis=0), ((1,), (0,)))
    high, low = halves(solved)
    for j, piece in enumerate((high, low, high)):
        right_own[2 * j * block:2 * (j + 1) * block, :] = piece
    right_copy = pltpu.make_async_copy(right_own, right, local_sem.at[0])
    right_copy.start()

    @pl.loop(done // 2, chunks // 2)
    def _(pair):
        solve_rows(pair)

    for i, owner, source in parts:
        @pl.when(p == owner)
        def _():
            for d in range(1, n_prow):
                pivot_copy(i, d, source).wait_send()

    for i in (0, 1):
        @pl.when(p == i)
        def _():
            for d in range(1, n_prow):
                shift_copy(i, d).wait_send()

    @pl.loop(0, PIECES)
    def _(piece):
        for s in (0, 1):
            for way, goes in enumerate(ways(s)):
                @pl.when(goes)
                def _():
                    cross_copy(s, piece, way).wait_send()

    @pl.loop(0, chunks)
    def _(k):
        sent(k)

    right_copy.wait()

    @pl.loop(0, chunks // 2)
    def _(pair):
        left_copy(pair).wait()


def update_kernel(n_prow, n_pcol, matrix, left, right, out):
    step = pl.program_id(0)
    blocks, size, col_blocks, _ = matrix.shape

    rows = left[...].reshape(blocks * size, 4 * size)
    rows = jnp.concatenate([rows[:, 0:2 * size], rows], axis=1)
    product = jnp.dot(rows, right[...], preferred_element_type=jnp.float32)
    product = product.reshape(blocks, size, col_blocks, size)
    p = lax.axis_index("prow")
    col = lax.broadcasted_iota(jnp.int32, (1, col_blocks, size), 1) * n_pcol
    cols_kept = col + lax.axis_index("pcol") >= 2
    for b in range(blocks):
        kept = cols_kept & ((step * blocks + b) * n_prow + p >= 2)
        out[b] = jnp.where(kept, matrix[b] - product[b], 0.0)


def on_device(n_prow, n_pcol, coupling, diagonal):
    chunks, size, col_blocks, _ = coupling.shape
    root = math.isqrt(n_prow)
    width = root if root * root == n_prow else n_prow
    f32 = jnp.float32
    dma = pltpu.SemaphoreType.DMA
    vmem = pl.BlockSpec(memory_space=pltpu.VMEM)
    left, right = pl.pallas_call(
        functools.partial(share_kernel, n_prow, n_pcol, width),
        out_shape=(
            jax.ShapeDtypeStruct((chunks, size, 4 * size), jnp.bfloat16),
            jax.ShapeDtypeStruct((6 * size, col_blocks * size), jnp.bfloat16),
        ),
        in_specs=[pl.BlockSpec(memory_space=pl.ANY), vmem],
        out_specs=(pl.BlockSpec(memory_space=pl.ANY),) * 2,
        scratch_shapes=[
            pltpu.VMEM((chunks, size, 4 * size), jnp.bfloat16),
            pltpu.VMEM((6 * size, col_blocks * size), jnp.bfloat16),
            pltpu.VMEM((2, chunks, size, size), f32),
            pltpu.VMEM((2 * size, 2 * size), f32),
            pltpu.VMEM((2, size, col_blocks, size), f32),
            pltpu.VMEM((3, size, size), f32),
            pltpu.VMEM((2, 8, size), f32),
            pltpu.VMEM((size, size), f32),
            pltpu.VMEM((size, size), f32),
            pltpu.VMEM(coupling.shape, f32),
            dma((chunks // 2,)), dma((chunks,)), dma((4,)), dma((chunks,)), dma((chunks,)), dma((chunks,)), dma((chunks,)),
            dma((3, n_prow)), dma((3,)), dma((3,)),
            dma((2, PIECES, 3)), dma((2, PIECES)), dma((2, n_prow)), dma((2,)),
        ],
        compiler_params=pltpu.CompilerParams(
            collective_id=0, has_side_effects=True, vmem_limit_bytes=60 * 1024 * 1024
        ),
        name="share_panels",
    )(coupling, diagonal)
    blocks = math.gcd(chunks, 4)
    return pl.pallas_call(
        functools.partial(update_kernel, n_prow, n_pcol),
        grid=(chunks // blocks,),
        out_shape=jax.ShapeDtypeStruct(coupling.shape, f32),
        in_specs=[
            pl.BlockSpec((blocks, size, col_blocks, size), lambda i: (i, 0, 0, 0)),
            pl.BlockSpec((blocks, size, 4 * size), lambda i: (i, 0, 0)),
            pl.BlockSpec((6 * size, col_blocks * size), lambda i: (0, 0)),
        ],
        out_specs=pl.BlockSpec((blocks, size, col_blocks, size), lambda i: (i, 0, 0, 0)),
        compiler_params=pltpu.CompilerParams(vmem_limit_bytes=60 * 1024 * 1024),
        name="update_trailing",
    )(coupling, left, right)


def solution(mesh):
    return jax.shard_map(
        functools.partial(on_device, mesh.shape["prow"], mesh.shape["pcol"]),
        mesh=mesh,
        in_specs=(P(None, "prow", None, "pcol"), P(None, "prow")),
        out_specs=P(None, "prow", None, "pcol"),
        check_vma=False,
    )
```

```python
import functools
import math

import jax
import jax.numpy as jnp
from jax import lax
from jax.experimental import pallas as pl
from jax.experimental.pallas import tpu as pltpu
from jax.sharding import PartitionSpec as P

HIGHEST = lax.Precision.HIGHEST
MESH = pl.DeviceIdType.MESH
GROUP = 8
PIECES = 4
SLOT = 2
QUICK = 6
CROSS = 2


def dot(a, b, contract):
    return lax.dot_general(
        a, b, (contract, ((), ())), precision=HIGHEST, preferred_element_type=jnp.float32
    )


def thirds(x):
    first = x.astype(jnp.bfloat16).astype(jnp.float32)
    rest = x - first
    second = rest.astype(jnp.bfloat16).astype(jnp.float32)
    return first, second, rest - second


def halves(x):
    high = x.astype(jnp.bfloat16)
    return high, (x - high.astype(jnp.float32)).astype(jnp.bfloat16)


def eliminate_group(work, group):
    size = work.shape[0]
    start = pl.multiple_of(group * GROUP, GROUP)
    lane = lax.broadcasted_iota(jnp.int32, (GROUP, size), 1) - start
    sub = lax.broadcasted_iota(jnp.int32, (GROUP, size), 0)
    rows = work[pl.ds(start, GROUP), :]
    cols = [
        jnp.broadcast_to(
            jnp.sum(jnp.where(lane == j, rows, 0.0), axis=1, keepdims=True), (GROUP, size)
        )
        for j in range(GROUP)
    ]
    own = (lane >= 0) & (lane < GROUP)
    rows = jnp.where(own, jnp.where(lane == sub, 1.0, 0.0), rows)
    for j in range(GROUP):
        scale = lax.rsqrt(cols[j][j:j + 1, :])
        row = rows[j:j + 1, :] * scale
        column = jnp.where(sub > j, cols[j] * scale, 0.0)
        rows = jnp.where(sub == j, row, rows - column * row)
        for m in range(j + 1, GROUP):
            cols[m] = cols[m] - column * (cols[m][j:j + 1, :] * scale)
    work[pl.ds(start, GROUP), :] = rows
    upper = jnp.where(lane >= GROUP, rows, 0.0)
    a1, a2, a3 = thirds(upper)
    b1, b2, b3 = thirds(rows)
    left = jnp.concatenate([a1, a1, a2, a2, a1, a3], axis=0).astype(jnp.bfloat16)
    right = jnp.concatenate([b1, b2, b1, b2, b3, b1], axis=0).astype(jnp.bfloat16)
    product = lax.dot_general(
        left, right, (((0,), (0,)), ((), ())), preferred_element_type=jnp.float32
    )
    lane_all = lax.broadcasted_iota(jnp.int32, (size, size), 1) - start
    row_all = lax.broadcasted_iota(jnp.int32, (size, size), 0) - start
    dead = (row_all >= GROUP) & (lane_all >= 0) & (lane_all < GROUP)
    work[...] = jnp.where(dead, 0.0, work[...]) - product


def lower_part(x):
    size = x.shape[0]
    row = lax.broadcasted_iota(jnp.int32, (size, size), 0)
    col = lax.broadcasted_iota(jnp.int32, (size, size), 1)
    return jnp.where(row >= col, x, 0.0)


def with_diagonal(block, shift_row):
    size = block.shape[0]
    row = lax.broadcasted_iota(jnp.int32, (size, size), 0)
    col = lax.broadcasted_iota(jnp.int32, (size, size), 1)
    return jnp.where(row == col, block + shift_row, block)


def share_kernel(
    n_prow, n_pcol, width, coupling, diagonal, left, right,
    left_own, right_own, panel, inverse, across, pivots, shift, work, below, stage,
    left_sem, stage_sem, local_sem, next_send, next_recv, mate_send, mate_recv,
    pivot_send, pivot_recv, pivot_local, cross_send, cross_recv, shift_send, shift_recv,
    first_send,
):
    p = lax.axis_index("prow")
    q = lax.axis_index("pcol")
    chunks, block = coupling.shape[:2]
    height = n_prow // width
    side = q % 2
    mate = q + 1 - 2 * side
    other = 1 - side
    y = p // width
    x = p % width

    barrier = pltpu.get_barrier_semaphore()
    for d in range(1, n_prow):
        pl.semaphore_signal(
            barrier, inc=1, device_id={"prow": (p + d) % n_prow}, device_id_type=MESH
        )
    pl.semaphore_signal(barrier, inc=1, device_id={"pcol": mate}, device_id_type=MESH)

    @pl.when(q >= 2)
    def _():
        pl.semaphore_signal(barrier, inc=1, device_id={"pcol": q - 2}, device_id_type=MESH)

    @pl.when(q + 2 < n_pcol)
    def _():
        pl.semaphore_signal(barrier, inc=1, device_id={"pcol": q + 2}, device_id_type=MESH)

    def staged(k):
        return pltpu.make_async_copy(coupling.at[k], stage.at[k], stage_sem.at[k])

    chips = n_pcol // 2
    for d in range(2, chips):
        @pl.when(q < 2)
        def _():
            pl.semaphore_signal(
                barrier, inc=1, device_id={"pcol": side + 2 * d}, device_id_type=MESH
            )

    @pl.when(q >= 4)
    def _():
        pl.semaphore_signal(barrier, inc=1, device_id={"pcol": side}, device_id_type=MESH)

    own_across = pltpu.make_async_copy(coupling.at[0], across.at[p % 2], local_sem.at[1])

    @pl.when(q < 2)
    def _():
        @pl.loop(0, chunks)
        def _(k):
            staged(k).start()

    @pl.when(p < 2)
    def _():
        own_across.start()

    @pl.when(p < 2)
    def _():
        own_across.wait()

    pl.semaphore_wait(
        barrier,
        n_prow + jnp.where(q >= 2, 1, 0) + jnp.where(q + 2 < n_pcol, 1, 0)
        + jnp.where(q < 2, max(chips - 2, 0), 0) + jnp.where(q >= 4, 1, 0),
    )

    def to_next(k):
        return pltpu.make_async_remote_copy(
            src_ref=panel.at[side, k], dst_ref=panel.at[side, k],
            send_sem=next_send.at[k], recv_sem=next_recv.at[k],
            device_id={"pcol": jnp.minimum(q + 2, n_pcol - 2 + side)}, device_id_type=MESH,
        )

    def to_mate(k):
        return pltpu.make_async_remote_copy(
            src_ref=panel.at[side, k], dst_ref=panel.at[side, k],
            send_sem=mate_send.at[k], recv_sem=mate_recv.at[k],
            device_id={"pcol": mate}, device_id_type=MESH,
        )

    def from_mate(k):
        return pltpu.make_async_remote_copy(
            src_ref=panel.at[other, k], dst_ref=panel.at[other, k],
            send_sem=mate_send.at[k], recv_sem=mate_recv.at[k],
            device_id={"pcol": mate}, device_id_type=MESH,
        )

    def forward(k):
        @pl.when(q < 2)
        def _():
            staged(k).wait()
            panel[side, k] = stage[k, :, 0, :]

        @pl.when(q >= 2)
        def _():
            to_next(k).wait_recv()

        @pl.when(q + 2 < n_pcol)
        def _():
            to_next(k).start()

        to_mate(k).start()

    def first_to(d):
        return pltpu.make_async_remote_copy(
            src_ref=panel.at[side, 0], dst_ref=panel.at[side, 0],
            send_sem=first_send.at[d], recv_sem=next_recv.at[0],
            device_id={"pcol": side + 2 * d}, device_id_type=MESH,
        )

    def forward_first():
        @pl.when(q < 2)
        def _():
            staged(0).wait()
            panel[side, 0] = stage[0, :, 0, :]

        @pl.when(q >= 2)
        def _():
            to_next(0).wait_recv()

        @pl.when((q < 2) & (p < 2))
        def _():
            for d in range(chips - 1, 0, -1):
                first_to(d).start()

        @pl.when((p >= 2) & (q + 2 < n_pcol))
        def _():
            to_next(0).start()

        to_mate(0).start()

    def sent_first():
        @pl.when((q < 2) & (p < 2))
        def _():
            for d in range(1, chips):
                first_to(d).wait_send()

        @pl.when((p >= 2) & (q + 2 < n_pcol))
        def _():
            to_next(0).wait_send()

        to_mate(0).wait_send()

    def sent(k):
        @pl.when(q + 2 < n_pcol)
        def _():
            to_next(k).wait_send()

        to_mate(k).wait_send()

    def pivot_copy(i, d, source):
        return pltpu.make_async_remote_copy(
            src_ref=panel.at[source, 0], dst_ref=pivots.at[i],
            send_sem=pivot_send.at[i, d], recv_sem=pivot_recv.at[i],
            device_id={"prow": (p + d) % n_prow}, device_id_type=MESH,
        )

    parts = ((0, 0, 0), (1, 1, 0), (2, 1, 1))

    def shift_copy(i, d):
        return pltpu.make_async_remote_copy(
            src_ref=diagonal.at[0:8], dst_ref=shift.at[i],
            send_sem=shift_send.at[i, d], recv_sem=shift_recv.at[i],
            device_id={"prow": (p + d) % n_prow}, device_id_type=MESH,
        )

    def shift_local(i):
        return pltpu.make_async_copy(diagonal.at[0:8], shift.at[i], local_sem.at[2 + i])

    def cross_copy(s, piece, way):
        rows = block // PIECES
        part = across.at[s, pl.ds(piece * rows, rows)]
        step = (width, 1, -1)[way]
        return pltpu.make_async_remote_copy(
            src_ref=part, dst_ref=part,
            send_sem=cross_send.at[s, piece, way], recv_sem=cross_recv.at[s, piece],
            device_id={"prow": (p + step + n_prow) % n_prow}, device_id_type=MESH,
        )

    def ways(s):
        return (
            (x == s) & (y + 1 < height),
            (x >= s) & (x + 1 < width),
            (x <= s) & (x >= 1),
        )

    def cross_start(s, piece):
        for way, goes in enumerate(ways(s)):
            @pl.when(goes)
            def _():
                cross_copy(s, piece, way).start()

    def passes_on(s):
        first, second, third = ways(s)
        return first | second | third

    def cross_relay(piece):
        for s in (0, 1):
            @pl.when((p != s) & passes_on(s))
            def _():
                cross_copy(s, piece, 0).wait_recv()
                cross_start(s, piece)

    def cross_end(piece):
        for s in (0, 1):
            @pl.when((p != s) & jnp.logical_not(passes_on(s)))
            def _():
                cross_copy(s, piece, 0).wait_recv()

    forward_first()
    for i in (0, 1):
        @pl.when(p == i)
        def _():
            for d in range(1, n_prow):
                shift_copy(i, d).start()
            shift_local(i).start()

    from_mate(0).wait_recv()
    for i, owner, source in parts:
        @pl.when(p == owner)
        def _():
            for d in range(1, n_prow):
                pivot_copy(i, d, source).start()
            pltpu.make_async_copy(panel.at[source, 0], pivots.at[i], pivot_local.at[i]).start()

    early = 1
    middle = (q >= 2) & (q + 2 < n_pcol)
    last = (q >= 2) & (q + 2 >= n_pcol)

    @pl.when(q < 2)
    def _():
        @pl.loop(early, chunks)
        def _(k):
            forward(k)

    def arrived(i, owner, source):
        @pl.when(p == owner)
        def _():
            pltpu.make_async_copy(panel.at[source, 0], pivots.at[i], pivot_local.at[i]).wait()

        @pl.when(p != owner)
        def _():
            pivot_copy(i, 1, source).wait_recv()

    def shift_arrived(i):
        @pl.when(p == i)
        def _():
            shift_local(i).wait()

        @pl.when(p != i)
        def _():
            shift_copy(i, 1).wait_recv()

    slots = block // (SLOT * GROUP)

    def pass_on(slot):
        k = early + jnp.where(slot < QUICK, slot, (slot + QUICK) // 2)

        @pl.when(middle & (k < chunks) & ((slot < QUICK) | (slot % 2 == 0)))
        def _():
            forward(k)

        for s in (0, 1):
            @pl.when((p == s) & (slot == CROSS))
            def _():
                @pl.loop(0, PIECES)
                def _(piece):
                    cross_start(s, piece)

        @pl.when((slot % 4 == 3) & (slot >= CROSS + 4))
        def _():
            cross_relay((slot - CROSS) // 4 - 1)

    def factor(i):
        @pl.loop(0, slots)
        def _(slot):
            pass_on(i * slots + slot)

            @pl.loop(0, SLOT)
            def _(part):
                eliminate_group(work, slot * SLOT + part)

        rows = slice(i * block, (i + 1) * block)
        inverse[rows, rows] = lower_part(work[...])
        return inverse[rows, rows]

    shift_arrived(0)
    arrived(*parts[0])
    work[...] = with_diagonal(pivots[0], shift[0, 0:1, :])
    first = factor(0)
    inverse[0:block, block:] = jnp.zeros_like(first)
    shift_arrived(1)
    arrived(*parts[1])
    arrived(*parts[2])
    below[...] = dot(pivots[1], first, ((1,), (1,)))
    work[...] = with_diagonal(pivots[2], shift[1, 0:1, :]) - dot(
        below[...], below[...], ((1,), (1,))
    )
    second = factor(1)
    done = min(early + (2 * slots + QUICK) // 2, chunks)

    def forward_middle(start, stop):
        for k in range(min(start, chunks), min(stop, chunks)):
            @pl.when(middle)
            def _():
                forward(k)

    relayed = (2 * slots - CROSS - 1) // 4
    forward_middle(done, done + 1)
    inverse[block:, 0:block] = -dot(
        second, dot(below[...], inverse[0:block, 0:block], ((1,), (0,))), ((1,), (0,))
    )

    @pl.loop(relayed, PIECES)
    def _(piece):
        cross_relay(piece)

    @pl.when(last)
    def _():
        @pl.loop(early, done)
        def _(k):
            forward(k)

    def left_copy(pair):
        part = pl.ds(2 * pair, 2)
        return pltpu.make_async_copy(left_own.at[part], left.at[part], left_sem.at[pair])

    def solve_rows(pair):
        @pl.when(middle & (pair + done + 1 < chunks))
        def _():
            forward(pair + done + 1)

        for k in (2 * pair, 2 * pair + 1):
            @pl.when(last & (k >= done))
            def _():
                forward(k)

            @pl.when(k > 0)
            def _():
                from_mate(k).wait_recv()

        raw = jnp.concatenate(
            [
                jnp.concatenate([panel[0, k], panel[1, k]], axis=1)
                for k in (2 * pair, 2 * pair + 1)
            ],
            axis=0,
        )
        solved_rows = jnp.concatenate(halves(dot(raw, inverse[...], ((1,), (1,)))), axis=1)
        left_own[2 * pair] = solved_rows[0:block]
        left_own[2 * pair + 1] = solved_rows[block:]
        left_copy(pair).start()

    @pl.loop(0, done // 2)
    def _(pair):
        solve_rows(pair)

    @pl.loop(0, PIECES)
    def _(piece):
        cross_end(piece)

    panels = [
        jnp.concatenate([across[s, :, c, :] for c in range(across.shape[2])], axis=1)
        for s in (0, 1)
    ]
    solved = dot(inverse[...], jnp.concatenate(panels, axis=0), ((1,), (0,)))
    high, low = halves(solved)
    for j, piece in enumerate((high, low, high)):
        right_own[2 * j * block:2 * (j + 1) * block, :] = piece
    right_copy = pltpu.make_async_copy(right_own, right, local_sem.at[0])
    right_copy.start()

    @pl.loop(done // 2, chunks // 2)
    def _(pair):
        solve_rows(pair)

    for i, owner, source in parts:
        @pl.when(p == owner)
        def _():
            for d in range(1, n_prow):
                pivot_copy(i, d, source).wait_send()

    for i in (0, 1):
        @pl.when(p == i)
        def _():
            for d in range(1, n_prow):
                shift_copy(i, d).wait_send()

    @pl.loop(0, PIECES)
    def _(piece):
        for s in (0, 1):
            for way, goes in enumerate(ways(s)):
                @pl.when(goes)
                def _():
                    cross_copy(s, piece, way).wait_send()

    sent_first()

    @pl.loop(1, chunks)
    def _(k):
        sent(k)

    right_copy.wait()

    @pl.loop(0, chunks // 2)
    def _(pair):
        left_copy(pair).wait()


def update_kernel(n_prow, n_pcol, matrix, left, right, out):
    step = pl.program_id(0)
    blocks, size, col_blocks, _ = matrix.shape

    rows = left[...].reshape(blocks * size, 4 * size)
    rows = jnp.concatenate([rows[:, 0:2 * size], rows], axis=1)
    product = jnp.dot(rows, right[...], preferred_element_type=jnp.float32)
    product = product.reshape(blocks, size, col_blocks, size)
    p = lax.axis_index("prow")
    col = lax.broadcasted_iota(jnp.int32, (1, col_blocks, size), 1) * n_pcol
    cols_kept = col + lax.axis_index("pcol") >= 2
    for b in range(blocks):
        kept = cols_kept & ((step * blocks + b) * n_prow + p >= 2)
        out[b] = jnp.where(kept, matrix[b] - product[b], 0.0)


def on_device(n_prow, n_pcol, coupling, diagonal):
    chunks, size, col_blocks, _ = coupling.shape
    root = math.isqrt(n_prow)
    width = root if root * root == n_prow else n_prow
    f32 = jnp.float32
    dma = pltpu.SemaphoreType.DMA
    vmem = pl.BlockSpec(memory_space=pltpu.VMEM)
    left, right = pl.pallas_call(
        functools.partial(share_kernel, n_prow, n_pcol, width),
        out_shape=(
            jax.ShapeDtypeStruct((chunks, size, 4 * size), jnp.bfloat16),
            jax.ShapeDtypeStruct((6 * size, col_blocks * size), jnp.bfloat16),
        ),
        in_specs=[pl.BlockSpec(memory_space=pl.ANY), vmem],
        out_specs=(pl.BlockSpec(memory_space=pl.ANY),) * 2,
        scratch_shapes=[
            pltpu.VMEM((chunks, size, 4 * size), jnp.bfloat16),
            pltpu.VMEM((6 * size, col_blocks * size), jnp.bfloat16),
            pltpu.VMEM((2, chunks, size, size), f32),
            pltpu.VMEM((2 * size, 2 * size), f32),
            pltpu.VMEM((2, size, col_blocks, size), f32),
            pltpu.VMEM((3, size, size), f32),
            pltpu.VMEM((2, 8, size), f32),
            pltpu.VMEM((size, size), f32),
            pltpu.VMEM((size, size), f32),
            pltpu.VMEM(coupling.shape, f32),
            dma((chunks // 2,)), dma((chunks,)), dma((4,)), dma((chunks,)), dma((chunks,)), dma((chunks,)), dma((chunks,)),
            dma((3, n_prow)), dma((3,)), dma((3,)),
            dma((2, PIECES, 3)), dma((2, PIECES)), dma((2, n_prow)), dma((2,)), dma((n_pcol // 2,)),
        ],
        compiler_params=pltpu.CompilerParams(
            collective_id=0, has_side_effects=True, vmem_limit_bytes=60 * 1024 * 1024
        ),
        name="share_panels",
    )(coupling, diagonal)
    blocks = math.gcd(chunks, 4)
    return pl.pallas_call(
        functools.partial(update_kernel, n_prow, n_pcol),
        grid=(chunks // blocks,),
        out_shape=jax.ShapeDtypeStruct(coupling.shape, f32),
        in_specs=[
            pl.BlockSpec((blocks, size, col_blocks, size), lambda i: (i, 0, 0, 0)),
            pl.BlockSpec((blocks, size, 4 * size), lambda i: (i, 0, 0)),
            pl.BlockSpec((6 * size, col_blocks * size), lambda i: (0, 0)),
        ],
        out_specs=pl.BlockSpec((blocks, size, col_blocks, size), lambda i: (i, 0, 0, 0)),
        compiler_params=pltpu.CompilerParams(vmem_limit_bytes=60 * 1024 * 1024),
        name="update_trailing",
    )(coupling, left, right)


def solution(mesh):
    return jax.shard_map(
        functools.partial(on_device, mesh.shape["prow"], mesh.shape["pcol"]),
        mesh=mesh,
        in_specs=(P(None, "prow", None, "pcol"), P(None, "prow")),
        out_specs=P(None, "prow", None, "pcol"),
        check_vma=False,
    )
```

```python
import functools
import math

import jax
import jax.numpy as jnp
from jax import lax
from jax.experimental import pallas as pl
from jax.experimental.pallas import tpu as pltpu
from jax.sharding import PartitionSpec as P

HIGHEST = lax.Precision.HIGHEST
MESH = pl.DeviceIdType.MESH
GROUP = 8
PIECES = 4
SLOT = 2
QUICK = 6
CROSS = 2


def dot(a, b, contract):
    return lax.dot_general(
        a, b, (contract, ((), ())), precision=HIGHEST, preferred_element_type=jnp.float32
    )


def thirds(x):
    first = x.astype(jnp.bfloat16).astype(jnp.float32)
    rest = x - first
    second = rest.astype(jnp.bfloat16).astype(jnp.float32)
    return first, second, rest - second


def halves(x):
    high = x.astype(jnp.bfloat16)
    return high, (x - high.astype(jnp.float32)).astype(jnp.bfloat16)


def eliminate_group(work, group):
    size = work.shape[0]
    start = pl.multiple_of(group * GROUP, GROUP)
    lane = lax.broadcasted_iota(jnp.int32, (GROUP, size), 1) - start
    sub = lax.broadcasted_iota(jnp.int32, (GROUP, size), 0)
    rows = work[pl.ds(start, GROUP), :]
    cols = [
        jnp.broadcast_to(
            jnp.sum(jnp.where(lane == j, rows, 0.0), axis=1, keepdims=True), (GROUP, size)
        )
        for j in range(GROUP)
    ]
    own = (lane >= 0) & (lane < GROUP)
    rows = jnp.where(own, jnp.where(lane == sub, 1.0, 0.0), rows)
    for j in range(GROUP):
        scale = lax.rsqrt(cols[j][j:j + 1, :])
        row = rows[j:j + 1, :] * scale
        column = jnp.where(sub > j, cols[j] * scale, 0.0)
        rows = jnp.where(sub == j, row, rows - column * row)
        for m in range(j + 1, GROUP):
            cols[m] = cols[m] - column * (cols[m][j:j + 1, :] * scale)
    work[pl.ds(start, GROUP), :] = rows
    upper = jnp.where(lane >= GROUP, rows, 0.0)
    a1, a2, a3 = thirds(upper)
    b1, b2, b3 = thirds(rows)
    left = jnp.concatenate([a1, a1, a2, a2, a1, a3], axis=0).astype(jnp.bfloat16)
    right = jnp.concatenate([b1, b2, b1, b2, b3, b1], axis=0).astype(jnp.bfloat16)
    product = lax.dot_general(
        left, right, (((0,), (0,)), ((), ())), preferred_element_type=jnp.float32
    )
    lane_all = lax.broadcasted_iota(jnp.int32, (size, size), 1) - start
    row_all = lax.broadcasted_iota(jnp.int32, (size, size), 0) - start
    dead = (row_all >= GROUP) & (lane_all >= 0) & (lane_all < GROUP)
    work[...] = jnp.where(dead, 0.0, work[...]) - product


def lower_part(x):
    size = x.shape[0]
    row = lax.broadcasted_iota(jnp.int32, (size, size), 0)
    col = lax.broadcasted_iota(jnp.int32, (size, size), 1)
    return jnp.where(row >= col, x, 0.0)


def with_diagonal(block, shift_row):
    size = block.shape[0]
    row = lax.broadcasted_iota(jnp.int32, (size, size), 0)
    col = lax.broadcasted_iota(jnp.int32, (size, size), 1)
    return jnp.where(row == col, block + shift_row, block)


def share_kernel(
    n_prow, n_pcol, width, coupling, diagonal, left, right,
    left_own, right_own, panel, inverse, across, pivots, shift, work, below, stage,
    left_sem, stage_sem, local_sem, next_send, next_recv, mate_send, mate_recv,
    pivot_send, pivot_recv, pivot_local, cross_send, cross_recv, shift_send, shift_recv,
):
    p = lax.axis_index("prow")
    q = lax.axis_index("pcol")
    chunks, block = coupling.shape[:2]
    height = n_prow // width
    side = q % 2
    mate = q + 1 - 2 * side
    other = 1 - side
    y = p // width
    x = p % width

    barrier = pltpu.get_barrier_semaphore()
    for d in range(1, n_prow):
        pl.semaphore_signal(
            barrier, inc=1, device_id={"prow": (p + d) % n_prow}, device_id_type=MESH
        )
    pl.semaphore_signal(barrier, inc=1, device_id={"pcol": mate}, device_id_type=MESH)

    @pl.when(q >= 2)
    def _():
        pl.semaphore_signal(barrier, inc=1, device_id={"pcol": q - 2}, device_id_type=MESH)

    @pl.when(q + 2 < n_pcol)
    def _():
        pl.semaphore_signal(barrier, inc=1, device_id={"pcol": q + 2}, device_id_type=MESH)

    def staged(k):
        return pltpu.make_async_copy(coupling.at[k], stage.at[k], stage_sem.at[k])

    own_across = pltpu.make_async_copy(coupling.at[0], across.at[p % 2], local_sem.at[1])

    @pl.when(q < 2)
    def _():
        @pl.loop(0, chunks)
        def _(k):
            staged(k).start()

    @pl.when(p < 2)
    def _():
        own_across.start()

    @pl.when(p < 2)
    def _():
        own_across.wait()

    pl.semaphore_wait(
        barrier,
        n_prow + jnp.where(q >= 2, 1, 0) + jnp.where(q + 2 < n_pcol, 1, 0),
    )

    def to_next(k):
        return pltpu.make_async_remote_copy(
            src_ref=panel.at[side, k], dst_ref=panel.at[side, k],
            send_sem=next_send.at[k], recv_sem=next_recv.at[k],
            device_id={"pcol": jnp.minimum(q + 2, n_pcol - 2 + side)}, device_id_type=MESH,
        )

    def to_mate(k):
        return pltpu.make_async_remote_copy(
            src_ref=panel.at[side, k], dst_ref=panel.at[side, k],
            send_sem=mate_send.at[k], recv_sem=mate_recv.at[k],
            device_id={"pcol": mate}, device_id_type=MESH,
        )

    def from_mate(k):
        return pltpu.make_async_remote_copy(
            src_ref=panel.at[other, k], dst_ref=panel.at[other, k],
            send_sem=mate_send.at[k], recv_sem=mate_recv.at[k],
            device_id={"pcol": mate}, device_id_type=MESH,
        )

    def forward(k):
        @pl.when(q < 2)
        def _():
            staged(k).wait()
            panel[side, k] = stage[k, :, 0, :]

        @pl.when(q >= 2)
        def _():
            to_next(k).wait_recv()

        @pl.when(q + 2 < n_pcol)
        def _():
            to_next(k).start()

        to_mate(k).start()

    def sent(k):
        @pl.when(q + 2 < n_pcol)
        def _():
            to_next(k).wait_send()

        to_mate(k).wait_send()

    def pivot_copy(i, d, source):
        return pltpu.make_async_remote_copy(
            src_ref=panel.at[source, 0], dst_ref=pivots.at[i],
            send_sem=pivot_send.at[i, d], recv_sem=pivot_recv.at[i],
            device_id={"prow": (p + d) % n_prow}, device_id_type=MESH,
        )

    parts = ((0, 0, 0), (1, 1, 0), (2, 1, 1))

    def shift_copy(i, d):
        return pltpu.make_async_remote_copy(
            src_ref=diagonal.at[0:8], dst_ref=shift.at[i],
            send_sem=shift_send.at[i, d], recv_sem=shift_recv.at[i],
            device_id={"prow": (p + d) % n_prow}, device_id_type=MESH,
        )

    def shift_local(i):
        return pltpu.make_async_copy(diagonal.at[0:8], shift.at[i], local_sem.at[2 + i])

    def cross_copy(s, piece, way):
        rows = block // PIECES
        part = across.at[s, pl.ds(piece * rows, rows)]
        step = (width, 1, -1)[way]
        return pltpu.make_async_remote_copy(
            src_ref=part, dst_ref=part,
            send_sem=cross_send.at[s, piece, way], recv_sem=cross_recv.at[s, piece],
            device_id={"prow": (p + step + n_prow) % n_prow}, device_id_type=MESH,
        )

    def ways(s):
        return (
            (x == s) & (y + 1 < height),
            (x >= s) & (x + 1 < width),
            (x <= s) & (x >= 1),
        )

    def cross_start(s, piece):
        for way, goes in enumerate(ways(s)):
            @pl.when(goes)
            def _():
                cross_copy(s, piece, way).start()

    def passes_on(s):
        first, second, third = ways(s)
        return first | second | third

    def cross_relay(piece):
        for s in (0, 1):
            @pl.when((p != s) & passes_on(s))
            def _():
                cross_copy(s, piece, 0).wait_recv()
                cross_start(s, piece)

    def cross_end(piece):
        for s in (0, 1):
            @pl.when((p != s) & jnp.logical_not(passes_on(s)))
            def _():
                cross_copy(s, piece, 0).wait_recv()

    forward(0)
    chunks_first = min(4, chunks)

    @pl.when(q < 2)
    def _():
        @pl.loop(1, chunks_first)
        def _(k):
            forward(k)

    for i in (0, 1):
        @pl.when(p == i)
        def _():
            for d in range(1, n_prow):
                shift_copy(i, d).start()
            shift_local(i).start()

    from_mate(0).wait_recv()
    for i, owner, source in parts:
        @pl.when(p == owner)
        def _():
            for d in range(1, n_prow):
                pivot_copy(i, d, source).start()
            pltpu.make_async_copy(panel.at[source, 0], pivots.at[i], pivot_local.at[i]).start()

    early = 1
    middle = (q >= 2) & (q + 2 < n_pcol)
    last = (q >= 2) & (q + 2 >= n_pcol)

    @pl.when(q < 2)
    def _():
        @pl.loop(chunks_first, chunks)
        def _(k):
            forward(k)

    def arrived(i, owner, source):
        @pl.when(p == owner)
        def _():
            pltpu.make_async_copy(panel.at[source, 0], pivots.at[i], pivot_local.at[i]).wait()

        @pl.when(p != owner)
        def _():
            pivot_copy(i, 1, source).wait_recv()

    def shift_arrived(i):
        @pl.when(p == i)
        def _():
            shift_local(i).wait()

        @pl.when(p != i)
        def _():
            shift_copy(i, 1).wait_recv()

    slots = block // (SLOT * GROUP)

    def pass_on(slot):
        k = early + jnp.where(slot < QUICK, slot, (slot + QUICK) // 2)

        @pl.when(middle & (k < chunks) & ((slot < QUICK) | (slot % 2 == 0)))
        def _():
            forward(k)

        for s in (0, 1):
            @pl.when((p == s) & (slot == CROSS))
            def _():
                @pl.loop(0, PIECES)
                def _(piece):
                    cross_start(s, piece)

        @pl.when((slot % 4 == 3) & (slot >= CROSS + 4))
        def _():
            cross_relay((slot - CROSS) // 4 - 1)

    def factor(i):
        @pl.loop(0, slots)
        def _(slot):
            pass_on(i * slots + slot)

            @pl.loop(0, SLOT)
            def _(part):
                eliminate_group(work, slot * SLOT + part)

        rows = slice(i * block, (i + 1) * block)
        inverse[rows, rows] = lower_part(work[...])
        return inverse[rows, rows]

    shift_arrived(0)
    arrived(*parts[0])
    work[...] = with_diagonal(pivots[0], shift[0, 0:1, :])
    first = factor(0)
    inverse[0:block, block:] = jnp.zeros_like(first)
    shift_arrived(1)
    arrived(*parts[1])
    arrived(*parts[2])
    below[...] = dot(pivots[1], first, ((1,), (1,)))
    work[...] = with_diagonal(pivots[2], shift[1, 0:1, :]) - dot(
        below[...], below[...], ((1,), (1,))
    )
    second = factor(1)
    done = min(early + (2 * slots + QUICK) // 2, chunks)

    def forward_middle(start, stop):
        for k in range(min(start, chunks), min(stop, chunks)):
            @pl.when(middle)
            def _():
                forward(k)

    relayed = (2 * slots - CROSS - 1) // 4
    forward_middle(done, done + 1)
    inverse[block:, 0:block] = -dot(
        second, dot(below[...], inverse[0:block, 0:block], ((1,), (0,))), ((1,), (0,))
    )

    @pl.loop(relayed, PIECES)
    def _(piece):
        cross_relay(piece)

    @pl.when(last)
    def _():
        @pl.loop(early, done)
        def _(k):
            forward(k)

    def left_copy(pair):
        part = pl.ds(2 * pair, 2)
        return pltpu.make_async_copy(left_own.at[part], left.at[part], left_sem.at[pair])

    def solve_rows(pair):
        @pl.when(middle & (pair + done + 1 < chunks))
        def _():
            forward(pair + done + 1)

        for k in (2 * pair, 2 * pair + 1):
            @pl.when(last & (k >= done))
            def _():
                forward(k)

            @pl.when(k > 0)
            def _():
                from_mate(k).wait_recv()

        raw = jnp.concatenate(
            [
                jnp.concatenate([panel[0, k], panel[1, k]], axis=1)
                for k in (2 * pair, 2 * pair + 1)
            ],
            axis=0,
        )
        solved_rows = jnp.concatenate(halves(dot(raw, inverse[...], ((1,), (1,)))), axis=1)
        left_own[2 * pair] = solved_rows[0:block]
        left_own[2 * pair + 1] = solved_rows[block:]
        left_copy(pair).start()

    @pl.loop(0, done // 2)
    def _(pair):
        solve_rows(pair)

    @pl.loop(0, PIECES)
    def _(piece):
        cross_end(piece)

    panels = [
        jnp.concatenate([across[s, :, c, :] for c in range(across.shape[2])], axis=1)
        for s in (0, 1)
    ]
    solved = dot(inverse[...], jnp.concatenate(panels, axis=0), ((1,), (0,)))
    high, low = halves(solved)
    for j, piece in enumerate((high, low, high)):
        right_own[2 * j * block:2 * (j + 1) * block, :] = piece
    right_copy = pltpu.make_async_copy(right_own, right, local_sem.at[0])
    right_copy.start()

    @pl.loop(done // 2, chunks // 2)
    def _(pair):
        solve_rows(pair)

    for i, owner, source in parts:
        @pl.when(p == owner)
        def _():
            for d in range(1, n_prow):
                pivot_copy(i, d, source).wait_send()

    for i in (0, 1):
        @pl.when(p == i)
        def _():
            for d in range(1, n_prow):
                shift_copy(i, d).wait_send()

    @pl.loop(0, PIECES)
    def _(piece):
        for s in (0, 1):
            for way, goes in enumerate(ways(s)):
                @pl.when(goes)
                def _():
                    cross_copy(s, piece, way).wait_send()

    @pl.loop(0, chunks)
    def _(k):
        sent(k)

    right_copy.wait()

    @pl.loop(0, chunks // 2)
    def _(pair):
        left_copy(pair).wait()


def update_kernel(n_prow, n_pcol, matrix, left, right, out):
    step = pl.program_id(0)
    blocks, size, col_blocks, _ = matrix.shape

    rows = left[...].reshape(blocks * size, 4 * size)
    rows = jnp.concatenate([rows[:, 0:2 * size], rows], axis=1)
    product = jnp.dot(rows, right[...], preferred_element_type=jnp.float32)
    product = product.reshape(blocks, size, col_blocks, size)
    p = lax.axis_index("prow")
    col = lax.broadcasted_iota(jnp.int32, (1, col_blocks, size), 1) * n_pcol
    cols_kept = col + lax.axis_index("pcol") >= 2
    for b in range(blocks):
        kept = cols_kept & ((step * blocks + b) * n_prow + p >= 2)
        out[b] = jnp.where(kept, matrix[b] - product[b], 0.0)


def on_device(n_prow, n_pcol, coupling, diagonal):
    chunks, size, col_blocks, _ = coupling.shape
    root = math.isqrt(n_prow)
    width = root if root * root == n_prow else n_prow
    f32 = jnp.float32
    dma = pltpu.SemaphoreType.DMA
    vmem = pl.BlockSpec(memory_space=pltpu.VMEM)
    left, right = pl.pallas_call(
        functools.partial(share_kernel, n_prow, n_pcol, width),
        out_shape=(
            jax.ShapeDtypeStruct((chunks, size, 4 * size), jnp.bfloat16),
            jax.ShapeDtypeStruct((6 * size, col_blocks * size), jnp.bfloat16),
        ),
        in_specs=[pl.BlockSpec(memory_space=pl.ANY), vmem],
        out_specs=(pl.BlockSpec(memory_space=pl.ANY),) * 2,
        scratch_shapes=[
            pltpu.VMEM((chunks, size, 4 * size), jnp.bfloat16),
            pltpu.VMEM((6 * size, col_blocks * size), jnp.bfloat16),
            pltpu.VMEM((2, chunks, size, size), f32),
            pltpu.VMEM((2 * size, 2 * size), f32),
            pltpu.VMEM((2, size, col_blocks, size), f32),
            pltpu.VMEM((3, size, size), f32),
            pltpu.VMEM((2, 8, size), f32),
            pltpu.VMEM((size, size), f32),
            pltpu.VMEM((size, size), f32),
            pltpu.VMEM(coupling.shape, f32),
            dma((chunks // 2,)), dma((chunks,)), dma((4,)), dma((chunks,)), dma((chunks,)), dma((chunks,)), dma((chunks,)),
            dma((3, n_prow)), dma((3,)), dma((3,)),
            dma((2, PIECES, 3)), dma((2, PIECES)), dma((2, n_prow)), dma((2,)),
        ],
        compiler_params=pltpu.CompilerParams(
            collective_id=0, has_side_effects=True, vmem_limit_bytes=60 * 1024 * 1024
        ),
        name="share_panels",
    )(coupling, diagonal)
    blocks = math.gcd(chunks, 4)
    return pl.pallas_call(
        functools.partial(update_kernel, n_prow, n_pcol),
        grid=(chunks // blocks,),
        out_shape=jax.ShapeDtypeStruct(coupling.shape, f32),
        in_specs=[
            pl.BlockSpec((blocks, size, col_blocks, size), lambda i: (i, 0, 0, 0)),
            pl.BlockSpec((blocks, size, 4 * size), lambda i: (i, 0, 0)),
            pl.BlockSpec((6 * size, col_blocks * size), lambda i: (0, 0)),
        ],
        out_specs=pl.BlockSpec((blocks, size, col_blocks, size), lambda i: (i, 0, 0, 0)),
        compiler_params=pltpu.CompilerParams(vmem_limit_bytes=60 * 1024 * 1024),
        name="update_trailing",
    )(coupling, left, right)


def solution(mesh):
    return jax.shard_map(
        functools.partial(on_device, mesh.shape["prow"], mesh.shape["pcol"]),
        mesh=mesh,
        in_specs=(P(None, "prow", None, "pcol"), P(None, "prow")),
        out_specs=P(None, "prow", None, "pcol"),
        check_vma=False,
    )
```
